256 devices in a mesh: dp: 8 (over z), mrow: 8 (over y_lo, x), mcol: 4 (over y_hi, core).
Axes of the slice: x: 4, y: 4 (y_hi: 2, y_lo: 2; y = y_hi * 2 + y_lo), z: 8, core: 2. Of those that a mesh axis runs over, the one named last changes fastest.
Arguments:
- weight: float32 [18432, 12288], P(('mrow', 'dp'), 'mcol'), may hold values from -8 to 8
- activations: bfloat16 [1536, 18432], P('dp', 'mrow'), may hold values from -80 to 80
- cotangent: bfloat16 [1536, 12288], P('dp', 'mcol'), may hold values from -10 to 10
- row_old: float32 [18432], replicated, may hold values from 0.1 to 1000
- col_old: float32 [12288], replicated, may hold values from 0.1 to 10
- next_input: bfloat16 [1536, 18432], P('dp', 'mrow'), may hold values from -6 to 6
Outputs:
- new_weight: float32 [18432, 12288], P(('mrow', 'dp'), 'mcol')
- row_factor: float32 [18432], P(('mrow', 'dp'))
- col_factor: float32 [12288], P('mcol')
- queries: float32 [1536, 12288], P(('dp', 'mrow'), 'mcol')
- scaled_step: float32 [18432, 12288], P(('mrow', 'dp'), 'mcol')
The draws below stay inside these ranges and needn't reach their ends.
All inputs are finite; a program needn't handle non-finite values.
Results may differ from the reference program's by a relative error of at most 0.0029.
Values may be sent and summed in bfloat16 or wider, within the bound.
A program may use at most 128 MiB of HBM per device.

```python
import math
import jax
import jax.numpy as jnp
from jax import lax

D = 18432
TOK_DEV = 192
QW = 12288
TOKENS = 1536
D_BLOCK = 2304
N_DP = 8


def rising(amount, top):
    frac = jnp.arange(amount, dtype=jnp.float32) / amount
    return (1.0 + (top - 1.0) * frac) * (2.0 / (1.0 + top))


def block_rising(top):
    frac = (jnp.arange(D) % D_BLOCK).astype(jnp.float32) / D_BLOCK
    return (1.0 + (top - 1.0) * frac) * (2.0 / (1.0 + top))


def draw_weight(key, part):
    key = jax.random.fold_in(key, 11)
    base = jnp.clip(jax.random.normal(key, (D, QW), jnp.float32), -5.0, 5.0)
    top = 3.0
    inner = 3.0
    scale = rising(D, top) * block_rising(inner)
    return jnp.clip(base * scale[:, None], -8.0, 8.0).astype(jnp.float32)


def draw_activations(key, part):
    key = jax.random.fold_in(key, 12)
    first, second = jax.random.split(key, 2)
    base = jnp.clip(jax.random.normal(first, (TOKENS, D), jnp.float32), -5.0, 5.0)
    spread = math.log(10.0)
    top = 3.0
    scales = jnp.exp(jax.random.uniform(second, (D,), jnp.float32, 0.0, spread)) * rising(D, top)
    return (base * scales[None, :]).astype(jnp.bfloat16)


def draw_cotangent(key, part):
    key = jax.random.fold_in(key, 13)
    first, second = jax.random.split(key, 2)
    base = jnp.clip(jax.random.normal(first, (TOKENS, QW), jnp.float32), -5.0, 5.0)
    spread = math.log(10.0)
    scales = jnp.exp(jax.random.uniform(second, (QW,), jnp.float32, 0.0, spread)) * TOKENS ** (-0.5)
    return jnp.clip(base * scales[None, :], -10.0, 10.0).astype(jnp.bfloat16)


def draw_row_old(key, part):
    key = jax.random.fold_in(key, 14)
    growth = math.log(30.0)
    noise = jnp.exp(jax.random.uniform(key, (D,), jnp.float32, math.log(0.1), math.log(10.0)))
    whole = jnp.arange(D, dtype=jnp.float32) / D
    inner = (jnp.arange(D) % D_BLOCK).astype(jnp.float32) / D_BLOCK
    lift = jnp.exp(growth * (0.5 * whole + 0.5 * inner))
    return jnp.clip(noise * lift * 0.1, 0.1, 1000.0).astype(jnp.float32)


def levels(own_key, extent, cuts, least, high):
    factor_of = 1.0
    for dim, shards_of in cuts:
        draws = jax.random.uniform(jax.random.fold_in(jax.random.fold_in(own_key, 6), dim), (shards_of,), jnp.float32, least / len(cuts), high / len(cuts))
        factor_of = factor_of * jnp.repeat(jnp.exp(draws), extent[dim] // shards_of).reshape((-1,) + (1,) * (len(extent) - 1 - dim))
    return factor_of


def scatter_about(rng, shape, width, limit, cuts=(), kind=jnp.bfloat16):
    level = levels(rng, shape, cuts, -0.22, 0.18) if cuts else 1.0
    array = jax.random.normal(rng, shape, jnp.float32) * width * level
    return jnp.minimum(jnp.maximum(array, -limit), limit).astype(kind)


def setup_inputs(seed: int = 0) -> dict:
    arg_keys = jax.random.split(jax.random.key(seed), 7)
    return {
        "weight": draw_weight(jax.random.fold_in(arg_keys[6], 71), 0),
        "activations": draw_activations(jax.random.fold_in(arg_keys[6], 71), 0),
        "cotangent": draw_cotangent(jax.random.fold_in(arg_keys[6], 71), 0),
        "row_old": draw_row_old(jax.random.fold_in(arg_keys[6], 71), 0),
        "col_old": jnp.clip(jnp.exp(jax.random.uniform(arg_keys[4], (QW,), jnp.float32, math.log(0.1), math.log(10.0))), 0.1, 10.0),
        "next_input": scatter_about(arg_keys[5], (TOKENS, D), 1.0, 6.0, ((0, 8), (1, 8))),
    }


SECOND_DECAY = 1.0 - 10.0 ** (-0.8)
SQUARE_EPS = 1e-30
STEP_RATE = 0.01

def reference(weight, activations, cotangent, row_old, col_old, next_input):

    def add_group(source, running):
        offset = (source * TOK_DEV).astype(jnp.int32)
        inputs = lax.dynamic_slice_in_dim(activations, offset, TOK_DEV, 0)
        grads_out = lax.dynamic_slice_in_dim(cotangent, offset, TOK_DEV, 0)
        product = lax.dot_general(inputs, grads_out, (((0,), (0,)), ((), ())), preferred_element_type=jnp.float32)
        return running + product
    grad = lax.fori_loop(0, N_DP, add_group, jnp.zeros((D, QW), jnp.float32))
    squares = grad * grad
    row_factor = SECOND_DECAY * row_old + (1.0 - SECOND_DECAY) * (lax.optimization_barrier(jnp.sum(squares, axis=1)) / QW + SQUARE_EPS)
    col_factor = SECOND_DECAY * col_old + (1.0 - SECOND_DECAY) * (lax.optimization_barrier(jnp.sum(squares, axis=0)) / D + SQUARE_EPS)
    row_mean = jnp.mean(row_factor)
    direction = grad / jnp.sqrt(row_factor[:, None] * col_factor[None, :] / row_mean)
    clip_factor = jnp.maximum(1.0, jnp.sqrt(jnp.mean(direction * direction)))
    weight_scale = jnp.sqrt(jnp.mean(weight * weight))
    scaled_step = weight_scale * direction / clip_factor
    new_weight = weight - STEP_RATE * scaled_step
    weight_half = new_weight.astype(jnp.bfloat16)
    summed = jnp.dot(next_input, weight_half, preferred_element_type=jnp.float32)
    queries = summed * D ** (-0.5)
    return (new_weight, row_factor, col_factor, queries, scaled_step)
```

```python
import jax
import jax.numpy as jnp
from jax import lax
from jax.experimental import pallas as pl
from jax.experimental.pallas import tpu as pltpu
from jax.sharding import PartitionSpec as P

SECOND_DECAY = 1.0 - 10.0 ** (-0.8)
SQUARE_EPS = 1e-30
STEP_RATE = 0.01

NZ = 8
NX = 4
TOK = 192
D = 18432
QW = 12288
TOKENS = 1536
FEAT = 288
BLOCK = 2304
COLS = 3072
HALF = 96
QTOK = 24
Z_COLS = 1024
X_BASE = 1024
X_COLS = 512
SLICE = COLS // NZ
CHUNK = 512
NCHUNK = COLS // CHUNK
SLOTS = 3
N_SEM = 256
MESH = pl.DeviceIdType.MESH
HI = lax.Precision.HIGHEST
F32 = jnp.float32
BF16 = jnp.bfloat16


def rot(base, step, size):
    return lax.rem(base + (step + size) % size, size)


def aligned(start, size, mult):
    return pl.ds(pl.multiple_of(start, mult), size)


def kernel(
    cot_hbm, act_hbm, nxt_hbm, w_hbm, row_old, row_mine, col_mine,
    g_out, q_out, rf_out, cf_out, sc_out,
    cot, grad, w_buf, act, act_s, act_all, act_t, nxt, nxt_s, nxt_y, nxt_all,
    row_acc, row_send, row_recv, vec, vec_z, vec_xy, scal, col_row,
    w_own, w_peer, part, opp_send, opp_recv, x_send, x_recv, z_send, z_recv,
    local_sem, send_sem, recv_sem,
):
    dp = lax.axis_index("dp")
    mr = lax.axis_index("mrow")
    mc = lax.axis_index("mcol")
    x = lax.rem(mr, NX)
    y = lax.div(mr, NX)
    core = lax.rem(mc, 2)
    sib = mc + 1 - 2 * core
    ymate = (1 - y) * NX + x
    count = [0]
    sent = []

    def remote(src, dst, dev):
        i = count[0]
        count[0] += 1
        return pltpu.make_async_remote_copy(
            src_ref=src, dst_ref=dst, send_sem=send_sem.at[i], recv_sem=recv_sem.at[i],
            device_id=dev, device_id_type=MESH,
        )

    def go(copy):
        copy.start()
        sent.append(copy)
        return copy

    def zdev(k):
        return {"dp": rot(dp, k, NZ)}

    def xdev(k):
        return {"mrow": y * NX + rot(x, k, NX)}

    def zrows(k):
        return aligned(rot(dp, k, NZ) * TOK, TOK, 64)

    own = zrows(0)
    loads = [
        pltpu.make_async_copy(cot_hbm, cot.at[own], local_sem.at[0]),
        pltpu.make_async_copy(act_hbm, act, local_sem.at[1]),
        pltpu.make_async_copy(nxt_hbm, nxt, local_sem.at[2]),
        pltpu.make_async_copy(w_hbm, w_buf, local_sem.at[3]),
    ]
    for load in loads:
        load.start()

    barrier = pltpu.get_barrier_semaphore()
    for k in range(1, NZ):
        pl.semaphore_signal(barrier, inc=1, device_id=zdev(k), device_id_type=MESH)
        pl.semaphore_signal(
            barrier, inc=1, device_id={"mrow": rot(mr, k, NZ)}, device_id_type=MESH
        )
    for k in range(1, 4):
        pl.semaphore_signal(
            barrier, inc=1, device_id={"mcol": rot(mc, k, 4)}, device_id_type=MESH
        )
    loads[0].wait()
    pl.semaphore_wait(barrier, 17)

    x_start = X_BASE + x * X_COLS
    flows = [
        (pl.multiple_of(x_start, 128), X_COLS, True),
        (0, Z_COLS // 2, False),
        (Z_COLS // 2, Z_COLS // 2, False),
    ]

    def z_send_step(flow, sign, s):
        start, width, _ = flow
        if s == 4:
            width = width // 2
            if sign < 0:
                start = start + width
        if not isinstance(start, int):
            start = pl.multiple_of(start, 128)
        ref = cot.at[zrows(-sign * (s - 1)), pl.ds(start, width)]
        return go(remote(ref, ref, zdev(sign)))

    step = {}
    for f, flow in enumerate(flows):
        for sign in (1, -1):
            step[f, sign, 1] = z_send_step(flow, sign, 1)

    loads[1].wait()
    for k in range(NZ):
        act_s[k] = act[:, k * FEAT:(k + 1) * FEAT]
    core_rows = pl.multiple_of(core * HALF, 32)
    act_in = {}
    for k in range(1, NZ):
        act_in[k] = go(remote(
            act_s.at[rot(dp, k, NZ), pl.ds(core_rows, HALF)],
            act_all.at[aligned(dp * TOK + core * HALF, HALF, 32)],
            zdev(k),
        ))
    act_all[own] = act_s[dp]

    loads[2].wait()
    for k in range(NZ):
        nxt_s[k] = nxt[:, k * FEAT:(k + 1) * FEAT]

    loads[3].wait()

    def weight_square(i, total):
        tile = w_buf[:, aligned(i * 256, 256, 256)]
        return total + jnp.sum((tile * tile).reshape(FEAT // 8, 8, 256), axis=0)

    wsq = lax.fori_loop(0, COLS // 256, weight_square, jnp.zeros((8, 256), F32))
    vec[...] = jnp.zeros((8, COLS), F32) + jnp.sum(wsq)

    def x_quarter(k, q, part_of, dev):
        width = X_COLS
        start = X_BASE + q * X_COLS
        if part_of is not None:
            width = X_COLS // 2
            start = start + part_of * width
        ref = cot.at[zrows(k), pl.ds(pl.multiple_of(start, 128), width)]
        return go(remote(ref, ref, dev))

    direct = {}
    forward = {}

    def x_piece(k):
        for sign in (1, -1):
            direct[k, sign] = x_quarter(k, x, None, xdev(sign))

    def x_forward(k):
        for sign in (1, -1):
            direct[k, sign].wait_recv()
            forward[k, sign] = x_quarter(k, rot(x, -sign, NX), 0 if sign > 0 else 1, xdev(sign))

    act_fwd = {}

    def act_forward(k):
        act_in[k].wait_recv()
        ref = act_all.at[aligned(rot(dp, -k, NZ) * TOK + core * HALF, HALF, 32)]
        act_fwd[k] = go(remote(ref, ref, {"mcol": sib}))

    for s in range(1, 5):
        for f, flow in enumerate(flows):
            for sign in (1, -1):
                step[f, sign, s].wait_recv()
                if s < 4:
                    step[f, sign, s + 1] = z_send_step(flow, sign, s + 1)
            if flow[2]:
                if s < 4:
                    x_piece(-s)
                    x_piece(s)
                else:
                    x_piece(4)
        if s > 1:
            x_forward(-(s - 1))
            x_forward(s - 1)
        if s == 2:
            for k in (1, 7, 2, 6):
                act_forward(k)
        if s == 3:
            for k in (3, 5, 4):
                act_forward(k)

    y_rows = pl.multiple_of(y * HALF, 32)
    o_rows = pl.multiple_of((1 - y) * HALF, 32)
    nxt_mate = go(remote(nxt_s.at[:, pl.ds(o_rows, HALF)], nxt_y, {"mrow": ymate}))
    nxt_in = {}
    for k in range(1, NZ):
        nxt_in[0, k] = go(remote(
            nxt_s.at[rot(dp, k, NZ), pl.ds(y_rows, HALF)],
            nxt_all.at[0, aligned(dp * HALF, HALF, 32)],
            zdev(k),
        ))
    nxt_all[0, aligned(dp * HALF, HALF, 32), :] = nxt_s[dp, pl.ds(y_rows, HALF), :]

    for k in range(1, NZ):
        act_fwd[k].wait_recv()
    for i in range(4):
        rows = slice(i * 384, (i + 1) * 384)
        act_t[:, rows] = act_all[rows, :].T
    row_acc[...] = jnp.zeros((FEAT, 128), F32)

    def grad_tiles(base, tiles):
        def one(i, carry):
            cols = aligned(base + i * 256, 256, 256)
            g = jnp.dot(act_t[...], cot[:, cols], preferred_element_type=F32)
            grad[:, cols] = g
            sq = g * g
            row_acc[...] += sq[:, :128] + sq[:, 128:]
            vec[0:1, cols] = jnp.sum(sq, axis=0, keepdims=True)
            return carry

        lax.fori_loop(0, tiles, one, 0)

    grad_tiles(0, Z_COLS // 256)
    grad_tiles(X_BASE + x * X_COLS, X_COLS // 256)
    x_forward(4)
    grad_tiles(X_BASE + rot(x, 1, NX) * X_COLS, X_COLS // 256)
    grad_tiles(X_BASE + rot(x, 3, NX) * X_COLS, X_COLS // 256)
    for k in (-1, 1, -2, 2, -3, 3, 4):
        for sign in (1, -1):
            forward[k, sign].wait_recv()
    grad_tiles(X_BASE + rot(x, 2, NX) * X_COLS, X_COLS // 256)
    g_copy = pltpu.make_async_copy(grad, g_out, local_sem.at[4])
    g_copy.start()

    ones = jnp.ones((8, 128), F32)
    row_send[...] = lax.dot_general(
        ones, row_acc[...], (((1,), (1,)), ((), ())), precision=HI, preferred_element_type=F32
    )
    row_in = [
        go(remote(row_send, row_recv.at[k], {"mcol": rot(mc, k, 4)})) for k in range(1, 4)
    ]
    nxt_mate.wait_recv()
    for k in range(1, NZ):
        nxt_in[1, k] = go(remote(
            nxt_y.at[rot(dp, k, NZ)],
            nxt_all.at[1, aligned(dp * HALF, HALF, 32)],
            zdev(k),
        ))
    nxt_all[1, aligned(dp * HALF, HALF, 32), :] = nxt_y[dp]
    for copy in row_in:
        copy.wait_recv()
    row_full = ((row_send[...] + row_recv[1]) + row_recv[2]) + row_recv[3]
    row_factor = SECOND_DECAY * row_mine[...] + (1.0 - SECOND_DECAY) * (
        row_full * (1.0 / QW) + SQUARE_EPS
    )
    rf_out[...] = row_factor[0:1]
    row_inv = lax.dot_general(
        1.0 / row_factor, ones * 0.125, (((0,), (0,)), ((), ())), precision=HI,
        preferred_element_type=F32,
    )
    row_root = jnp.sqrt(row_inv)

    def weighted(i, carry):
        cols = aligned(i * 256, 256, 256)
        g = grad[:, cols]
        vec[1:2, cols] = jnp.sum(g * g * row_inv[:, 0:1], axis=0, keepdims=True)
        return carry

    lax.fori_loop(0, COLS // 256, weighted, 0)

    def vslice(k):
        return aligned(rot(dp, k, NZ) * SLICE, SLICE, 128)

    z_in = [
        go(remote(vec.at[:, vslice(k)], vec_z.at[k], zdev(k))) for k in range(1, NZ)
    ]
    total = vec[:, vslice(0)]
    for k in range(1, NZ):
        z_in[k - 1].wait_recv()
        total = total + vec_z[k]
    vec_xy[0] = total
    xy_in = [
        go(remote(vec_xy.at[0], vec_xy.at[k], {"mrow": rot(mr, k, NZ)}))
        for k in range(1, NZ)
    ]
    for k in range(1, NZ):
        xy_in[k - 1].wait_recv()
        total = total + vec_xy[k]
    vec_z[0] = total
    full_in = []
    for k in range(1, NZ):
        full_in.append(go(remote(vec_z.at[0], scal.at[0, :, vslice(0)], zdev(k))))
    scal[0, :, vslice(0)] = total
    for copy in full_in:
        copy.wait_recv()
    col_factor = SECOND_DECAY * col_mine[...] + (1.0 - SECOND_DECAY) * (
        scal[0, 0:1, :] * (1.0 / D) + SQUARE_EPS
    )
    cf_out[...] = col_factor
    square_total = jnp.sum(scal[0, 0:1, :])
    update_total = jnp.sum(scal[0, 1:2, :] / col_factor)
    w_total = scal[0, 2:3, 0:128]
    scal[1, 0:1, 0:128] = jnp.zeros((1, 128), F32) + square_total
    scal[1, 1:2, 0:128] = jnp.zeros((1, 128), F32) + update_total
    scal[1, 2:3, 0:128] = w_total
    scal[1, 3:8, 0:128] = jnp.zeros((5, 128), F32)
    s_in = [
        go(remote(
            scal.at[1, :, pl.ds(0, 128)], scal.at[1, :, pl.ds(k * 128, 128)],
            {"mcol": rot(mc, k, 4)},
        ))
        for k in range(1, 4)
    ]
    old_total = jnp.sum(row_old[...])
    for copy in s_in:
        copy.wait_recv()
    sums = (
        (scal[1, :, 0:128] + scal[1, :, 128:256]) + scal[1, :, 256:384]
    ) + scal[1, :, 384:512]
    row_mean = (
        SECOND_DECAY * old_total
        + (1.0 - SECOND_DECAY) * (sums[0:1] * (1.0 / QW) + D * SQUARE_EPS)
    ) * (1.0 / D)
    entries = float(D) * float(QW)
    clip = jnp.maximum(1.0, jnp.sqrt(row_mean * sums[1:2] * (1.0 / entries)))
    w_scale = jnp.sqrt(sums[2:3] * (1.0 / entries))
    scale = w_scale * jnp.sqrt(row_mean) / clip
    sc_out[...] = jnp.zeros((8, 128), F32) + scale
    col_scale = (STEP_RATE * scale[0:1, 0:1]) * lax.rsqrt(col_factor)

    col_row[...] = col_scale
    w_in = []
    for c in range(NCHUNK):
        def update(i, carry, c=c):
            cols = aligned(c * CHUNK + i * 256, 256, 256)
            new_w = w_buf[:, cols] - grad[:, cols] * (row_root[:, 0:1] * col_row[0:1, cols])
            w_own[:, cols] = new_w.astype(BF16)
            return carry

        lax.fori_loop(0, CHUNK // 256, update, 0)
        cols = pl.ds(c * CHUNK, CHUNK)
        w_in.append(go(remote(w_own.at[:, cols], w_peer.at[:, cols], {"mrow": ymate})))
    for copy in nxt_in.values():
        copy.wait_recv()

    opp_in = {}
    x_in = {}
    z_part = {}
    x_next = rot(x, 1, NX)
    x_prev = rot(x, 3, NX)
    x_opp = rot(x, 2, NX)
    hw = CHUNK // 2

    def block(c, q, cols=slice(None)):
        return part[c % SLOTS, :, q, :, cols].reshape(NZ * QTOK, -1)

    def stage_matmul(c):
        w_in[c].wait_recv()

        def one(i, carry):
            src = aligned(c * CHUNK + i * 256, 256, 256)
            for r in range(2):
                rows = slice(r * 384, (r + 1) * 384)
                p = jnp.dot(nxt_all[0, rows, :], w_own[:, src], preferred_element_type=F32)
                p = p + jnp.dot(nxt_all[1, rows, :], w_peer[:, src], preferred_element_type=F32)
                part[c % SLOTS, r * 4:(r + 1) * 4, :, :, aligned(i * 256, 256, 256)] = (
                    p.reshape(4, NX, QTOK, 256)
                )
            return carry

        lax.fori_loop(0, CHUNK // 256, one, 0)
        opp_send[c, 0] = block(c, x_opp, slice(0, hw)).astype(BF16)
        opp_send[c, 1] = block(c, x_opp, slice(hw, CHUNK)).astype(BF16)
        for j, sign in ((0, 1), (1, -1)):
            opp_in[c, j] = go(remote(opp_send.at[c, j], opp_recv.at[c, j], xdev(sign)))

    def stage_relay(c):
        opp_in[c, 0].wait_recv()
        x_send[c, 0, :, 0:hw] = (
            block(c, x_next, slice(0, hw)) + opp_recv[c, 0].astype(F32)
        ).astype(BF16)
        x_send[c, 0, :, hw:CHUNK] = block(c, x_next, slice(hw, CHUNK)).astype(BF16)
        x_in[c, 0] = go(remote(x_send.at[c, 0], x_recv.at[c, 0], xdev(1)))
        opp_in[c, 1].wait_recv()
        x_send[c, 1, :, hw:CHUNK] = (
            block(c, x_prev, slice(hw, CHUNK)) + opp_recv[c, 1].astype(F32)
        ).astype(BF16)
        x_send[c, 1, :, 0:hw] = block(c, x_prev, slice(0, hw)).astype(BF16)
        x_in[c, 1] = go(remote(x_send.at[c, 1], x_recv.at[c, 1], xdev(-1)))

    def stage_z(c):
        x_in[c, 0].wait_recv()
        x_in[c, 1].wait_recv()
        summed = (
            block(c, x) + x_recv[c, 0].astype(F32) + x_recv[c, 1].astype(F32)
        ).reshape(NZ, QTOK, CHUNK)
        part[c % SLOTS, :, x, :, :] = summed
        z_send[c] = jnp.concatenate(
            [summed[:, :, :hw], summed[:, :, hw:]], axis=1
        ).astype(BF16)
        for k in range(1, NZ):
            z_part[c, k] = go(remote(
                z_send.at[c, rot(dp, k, NZ)], z_recv.at[c, k], zdev(k)
            ))
        q_out[:, c * CHUNK:(c + 1) * CHUNK] = part[c % SLOTS, dp, x, :, :]

    def stage_out(c):
        acc = None
        for k in range(1, NZ):
            z_part[c, k].wait_recv()
            term = z_recv[c, k].astype(F32)
            acc = term if acc is None else acc + term
        for j in range(2):
            cols = slice(c * CHUNK + j * hw, c * CHUNK + (j + 1) * hw)
            q_out[:, cols] = (q_out[:, cols] + acc[j * QTOK:(j + 1) * QTOK]) * D ** (-0.5)

    for t in range(NCHUNK + 3):
        if t < NCHUNK:
            stage_matmul(t)
        if 0 <= t - 1 < NCHUNK:
            stage_relay(t - 1)
        if 0 <= t - 2 < NCHUNK:
            stage_z(t - 2)
        if 0 <= t - 3 < NCHUNK:
            stage_out(t - 3)

    g_copy.wait()
    for copy in sent:
        copy.wait_send()


def body(weight, activations, cotangent, row_old, col_old, next_input):
    row_base = (lax.axis_index("mrow") * NZ + lax.axis_index("dp")) * FEAT
    col_base = lax.axis_index("mcol") * COLS
    row_mine = lax.dynamic_slice(row_old, (row_base,), (FEAT,)).reshape(1, FEAT)
    col_mine = lax.dynamic_slice(col_old, (col_base,), (COLS,)).reshape(1, COLS)
    vm = pl.BlockSpec(memory_space=pltpu.VMEM)
    hbm = pl.BlockSpec(memory_space=pl.ANY)
    v = pltpu.VMEM
    grad, queries, row_factor, col_factor, scale = pl.pallas_call(
        kernel,
        out_shape=(
            jax.ShapeDtypeStruct((FEAT, COLS), F32),
            jax.ShapeDtypeStruct((QTOK, COLS), F32),
            jax.ShapeDtypeStruct((1, FEAT), F32),
            jax.ShapeDtypeStruct((1, COLS), F32),
            jax.ShapeDtypeStruct((8, 128), F32),
        ),
        in_specs=[hbm, hbm, hbm, hbm, vm, vm, vm],
        out_specs=(hbm, vm, vm, vm, vm),
        scratch_shapes=[
            v((TOKENS, COLS), BF16),
            v((FEAT, COLS), F32),
            v((FEAT, COLS), F32),
            v((TOK, BLOCK), BF16),
            v((NZ, TOK, FEAT), BF16),
            v((TOKENS, FEAT), BF16),
            v((FEAT, TOKENS), BF16),
            v((TOK, BLOCK), BF16),
            v((NZ, TOK, FEAT), BF16),
            v((NZ, HALF, FEAT), BF16),
            v((2, TOKENS // 2, FEAT), BF16),
            v((FEAT, 128), F32),
            v((8, FEAT), F32),
            v((4, 8, FEAT), F32),
            v((8, COLS), F32),
            v((NZ, 8, SLICE), F32),
            v((NZ, 8, SLICE), F32),
            v((2, 8, COLS), F32),
            v((1, COLS), F32),
            v((FEAT, COLS), BF16),
            v((FEAT, COLS), BF16),
            v((SLOTS, NZ, NX, QTOK, CHUNK), F32),
            v((NCHUNK, 2, TOK, CHUNK // 2), BF16),
            v((NCHUNK, 2, TOK, CHUNK // 2), BF16),
            v((NCHUNK, 2, TOK, CHUNK), BF16),
            v((NCHUNK, 2, TOK, CHUNK), BF16),
            v((NCHUNK, NZ, 2 * QTOK, CHUNK // 2), BF16),
            v((NCHUNK, NZ, 2 * QTOK, CHUNK // 2), BF16),
            pltpu.SemaphoreType.DMA((5,)),
            pltpu.SemaphoreType.DMA((N_SEM,)),
            pltpu.SemaphoreType.DMA((N_SEM,)),
        ],
        compiler_params=pltpu.CompilerParams(
            collective_id=0, has_side_effects=True, vmem_limit_bytes=60 * 1024 * 1024
        ),
        cost_estimate=pl.CostEstimate(
            flops=4 * TOKENS * FEAT * COLS, bytes_accessed=16_000_000, transcendentals=0
        ),
        name="update",
    )(
        cotangent, activations, next_input, weight,
        row_old.reshape(D // 128, 128), row_mine, col_mine,
    )
    row_factor = row_factor.reshape(FEAT)
    col_factor = col_factor.reshape(COLS)
    factor = scale[0, 0] * lax.rsqrt(row_factor)
    scaled_step = grad * (factor[:, None] * lax.rsqrt(col_factor)[None, :])
    new_weight = weight - STEP_RATE * scaled_step
    return (new_weight, row_factor, col_factor, queries, scaled_step)


def solution(mesh):
    placed = (
        P(("mrow", "dp"), "mcol"),
        P("dp", "mrow"),
        P("dp", "mcol"),
        P(),
        P(),
        P("dp", "mrow"),
    )
    return jax.shard_map(
        body,
        mesh=mesh,
        in_specs=placed,
        out_specs=(
            P(("mrow", "dp"), "mcol"),
            P(("mrow", "dp")),
            P("mcol"),
            P(("dp", "mrow"), "mcol"),
            P(("mrow", "dp"), "mcol"),
        ),
        check_vma=False,
    )
```

```python
import jax
import jax.numpy as jnp
from jax import lax
from jax.experimental import pallas as pl
from jax.experimental.pallas import tpu as pltpu
from jax.sharding import PartitionSpec as P

SECOND_DECAY = 1.0 - 10.0 ** (-0.8)
SQUARE_EPS = 1e-30
STEP_RATE = 0.01

NZ = 8
NX = 4
PLANE = 32
TOK = 192
D = 18432
QW = 12288
TOKENS = 1536
FEAT = 288
BLOCK = 2304
COLS = 3072
HALF = 96
QTOK = 24
B_COLS = 128
E_BASE = 512
E_COLS = 768
H_BASE = 2048
H_COLS = 256
WIDTHS = (256, 256, 512, 512, 512, 512, 256, 256)
STARTS = tuple(sum(WIDTHS[:i]) for i in range(len(WIDTHS)))
NCHUNK = len(WIDTHS)
WMAX = max(WIDTHS)
SLOTS = 4
N_SEM = 320
MESH = pl.DeviceIdType.MESH
HI = lax.Precision.HIGHEST
F32 = jnp.float32
BF16 = jnp.bfloat16


def rot(base, step, size):
    return lax.rem(base + (step + size) % size, size)


def aligned(start, size, mult):
    return pl.ds(pl.multiple_of(start, mult), size)


def kernel(
    cot_hbm, act_hbm, nxt_hbm, w_hbm, row_old, col_old,
    w_out, s_out, q_out, rf_out, cf_out,
    rs_buf, cs_buf, cot, grad, w_buf, act, act_s, act_all, act_t, nxt, nxt_s, nxt_y, nxt_all,
    row_acc, row_send, row_recv, vec, vec_z, vec_xy, col_all, scal,
    w_own, w_peer, part, opp_send, opp_recv, x_send, x_recv, z_send, z_recv,
    local_sem, send_sem, recv_sem,
):
    dp = lax.axis_index("dp")
    mr = lax.axis_index("mrow")
    mc = lax.axis_index("mcol")
    x = lax.rem(mr, NX)
    y = lax.div(mr, NX)
    core = lax.rem(mc, 2)
    sib = {"mcol": mc + 1 - 2 * core}
    ymate = {"mrow": (1 - y) * NX + x}
    count = [0]
    sent = []

    def remote(src, dst, dev):
        i = count[0]
        count[0] += 1
        copy = pltpu.make_async_remote_copy(
            src_ref=src, dst_ref=dst, send_sem=send_sem.at[i], recv_sem=recv_sem.at[i],
            device_id=dev, device_id_type=MESH,
        )
        copy.start()
        sent.append(copy)
        return copy

    def zdev(k):
        return {"dp": rot(dp, k, NZ)}

    def pdev(k):
        place = rot(mr * 4 + mc, k, PLANE)
        return {"mrow": lax.div(place, 4), "mcol": lax.rem(place, 4)}

    def xdev(k):
        return {"mrow": y * NX + rot(x, k, NX)}

    def zrows(k, half=None):
        if half is None:
            return aligned(rot(dp, k, NZ) * TOK, TOK, 64)
        return aligned(rot(dp, k, NZ) * TOK + half * HALF, HALF, 32)

    loads = [
        pltpu.make_async_copy(act_hbm, act, local_sem.at[0]),
        pltpu.make_async_copy(cot_hbm, cot.at[zrows(0)], local_sem.at[1]),
        pltpu.make_async_copy(nxt_hbm, nxt, local_sem.at[2]),
        pltpu.make_async_copy(w_hbm, w_buf, local_sem.at[3]),
    ]
    for load in loads:
        load.start()

    barrier = pltpu.get_barrier_semaphore()
    for k in range(1, NZ):
        pl.semaphore_signal(barrier, inc=1, device_id=zdev(k), device_id_type=MESH)
    for k in range(1, PLANE):
        pl.semaphore_signal(barrier, inc=1, device_id=pdev(k), device_id_type=MESH)
    loads[0].wait()
    for k in range(NZ):
        act_s[k] = act[:, k * FEAT:(k + 1) * FEAT]
    loads[1].wait()
    loads[2].wait()
    for k in range(NZ):
        nxt_s[k] = nxt[:, k * FEAT:(k + 1) * FEAT]
    pl.semaphore_wait(barrier, NZ + PLANE - 2)

    q_rows = HALF // 2
    nxt_mate = remote(
        nxt_s.at[:, aligned((1 - y) * HALF + core * q_rows, q_rows, 16)], nxt_y, ymate
    )

    even = lax.rem(x, 2)
    flows = {
        "h": (H_BASE + (2 * y + even) * H_COLS, H_COLS),
        "b": (x * B_COLS, B_COLS),
        "e": (E_BASE + even * E_COLS, E_COLS // 2),
        "f": (E_BASE + even * E_COLS + E_COLS // 2, E_COLS // 2),
    }
    moves = {"h": (1 - 2 * even) * H_COLS, "e": (1 - 2 * even) * E_COLS}
    moves["f"] = moves["e"]
    z_in = {}

    def z_step(f, s):
        start, width = flows[f]
        cols = aligned(start, width, 128)
        for sign in (1, -1):
            half = None if s < 4 else (1 - sign) // 2
            ref = cot.at[zrows(-sign * (s - 1), half), cols]
            z_in[f, sign, s] = remote(ref, ref, zdev(sign))

    def z_next(f, s):
        for sign in (1, -1):
            z_in[f, sign, s].wait_recv()
        if s < 4:
            z_step(f, s + 1)

    def pieces(s):
        return (4,) if s == 4 else (-s, s)

    x_in = {}
    b_in = {}
    y_in = {}

    def x_ref(k, f, half):
        start, width = flows[f]
        return cot.at[zrows(k, half), aligned(start, width, 128)]

    def x_send_pair(f, k):
        for sign in (1, -1):
            ref = x_ref(k, f, (1 - sign) // 2)
            x_in[f, k, sign] = remote(ref, ref, xdev(sign))

    def b_direct(k):
        for sign in (1, -1):
            ref = x_ref(k, "b", None)
            x_in["b", k, sign] = remote(ref, ref, xdev(sign))

    def b_forward(k):
        for sign in (1, -1):
            x_in["b", k, sign].wait_recv()
            ref = cot.at[
                zrows(k, (1 - sign) // 2), aligned(rot(x, -sign, NX) * B_COLS, B_COLS, 128)
            ]
            b_in[k, sign] = remote(ref, ref, xdev(sign))

    def y_own(k):
        ref = x_ref(k, "h", None)
        y_in[k, 0] = remote(ref, ref, ymate)

    def y_other(k):
        for sign in (1, -1):
            x_in["h", k, sign].wait_recv()
        ref = cot.at[zrows(k), aligned(flows["h"][0] + moves["h"], H_COLS, 128)]
        y_in[k, 1] = remote(ref, ref, ymate)

    core_rows = aligned(core * HALF, HALF, 32)
    act_in = {}
    act_fwd = {}

    def act_forward(k):
        act_in[k].wait_recv()
        ref = act_all.at[zrows(-k, core)]
        act_fwd[k] = remote(ref, ref, sib)

    def act_send(k):
        act_in[k] = remote(
            act_s.at[rot(dp, k, NZ), core_rows], act_all.at[zrows(0, core)], zdev(k)
        )

    for f in ("h", "b", "e", "f"):
        z_step(f, 1)
    for s in range(1, 5):
        z_next("h", s)
        for k in pieces(s):
            x_send_pair("h", k)
            y_own(k)
        z_next("b", s)
        for k in pieces(s):
            b_direct(k)
        if s == 1:
            for k in (4, 3, 5):
                act_send(k)
            act_all[zrows(0), :] = act_s[dp]
            loads[3].wait()

            def weight_square(i, total):
                tile = w_buf[:, aligned(i * 256, 256, 256)]
                return total + jnp.sum((tile * tile).reshape(FEAT // 8, 8, 256), axis=0)

            wsq = lax.fori_loop(0, COLS // 256, weight_square, jnp.zeros((8, 256), F32))
            vec[...] = jnp.zeros((NZ, 8, 128), F32) + jnp.sum(wsq)
            row_acc[...] = jnp.zeros((FEAT, 128), F32)
        if s == 2:
            for k in (2, 6, 1, 7):
                act_send(k)
        if s > 1:
            for k in pieces(s - 1):
                y_other(k)
                b_forward(k)
        if s == 3:
            for k in (4, 3, 5):
                act_forward(k)
        if s == 4:
            for k in (2, 6, 1, 7):
                act_forward(k)
        for f in ("e", "f"):
            z_next(f, s)
            for k in pieces(s):
                x_send_pair(f, k)

    def nxt_part(z, j):
        return nxt_all.at[j, z, aligned(core * q_rows, q_rows, 16)]

    mine = aligned(y * HALF + core * q_rows, q_rows, 16)
    nxt_mate.wait_recv()
    nxt_in = {}
    for k in range(1, NZ):
        nxt_in[0, k] = remote(nxt_s.at[rot(dp, k, NZ), mine], nxt_part(dp, 0), zdev(k))
        nxt_in[1, k] = remote(nxt_y.at[rot(dp, k, NZ)], nxt_part(dp, 1), zdev(k))
    nxt_part(dp, 0)[...] = nxt_s[dp, mine, :]
    nxt_part(dp, 1)[...] = nxt_y[dp]

    for k in range(1, NZ):
        act_fwd[k].wait_recv()
    for i in range(4):
        rows = slice(i * 384, (i + 1) * 384)
        act_t[:, rows] = act_all[rows, :].T
    y_other(4)
    b_forward(4)

    def grad_tiles(base, tiles):
        def one(i, carry):
            start = base + i * 256
            cols = aligned(start, 256, 256)
            g = jnp.dot(act_t[...], cot[:, cols], preferred_element_type=F32)
            grad[:, cols] = g
            sq = g * g
            row_acc[...] += sq[:, :128] + sq[:, 128:]
            sums = jnp.sum(sq, axis=0, keepdims=True)
            for j in range(2):
                block = lax.div(start, 128) + j
                vec[lax.div(block, 3), pl.ds(lax.rem(block, 3), 1), :] = (
                    sums[:, j * 128:(j + 1) * 128]
                )
            return carry

        lax.fori_loop(0, tiles, one, 0)

    every = (-1, 1, -2, 2, -3, 3, 4)
    grad_tiles(H_BASE + y * 2 * H_COLS, 2 * H_COLS // 256)
    for k in every:
        for sign in (1, -1):
            b_in[k, sign].wait_recv()
    grad_tiles(0, NX * B_COLS // 256)
    grad_tiles(flows["e"][0], E_COLS // 256)
    for k in every:
        for j in range(2):
            y_in[k, j].wait_recv()
    grad_tiles(H_BASE + (1 - y) * 2 * H_COLS, 2 * H_COLS // 256)
    for k in every:
        for sign in (1, -1):
            x_in["e", k, sign].wait_recv()
            x_in["f", k, sign].wait_recv()
    grad_tiles(flows["e"][0] + moves["e"], E_COLS // 256)

    ones = jnp.ones((8, 128), F32)
    row_send[...] = lax.dot_general(
        ones, row_acc[...], (((1,), (1,)), ((), ())), precision=HI, preferred_element_type=F32
    )
    row_in = [
        remote(row_send, row_recv.at[k], {"mcol": rot(mc, k, 4)}) for k in range(1, 4)
    ]
    place = (mr * NZ + dp) * (FEAT // 32)
    first = lax.div(place, 4)
    shift = lax.rem(place, 4)
    near = jnp.concatenate([row_old[pl.ds(first + j, 1), :] for j in range(3)], axis=1)
    row_mine = near[:, 0:FEAT]
    for j in range(1, 4):
        row_mine = jnp.where(shift == j, near[:, j * 32:j * 32 + FEAT], row_mine)
    for copy in row_in:
        copy.wait_recv()
    row_full = ((row_send[...] + row_recv[1]) + row_recv[2]) + row_recv[3]
    row_factor = SECOND_DECAY * row_mine + (1.0 - SECOND_DECAY) * (
        row_full * (1.0 / QW) + SQUARE_EPS
    )
    rf_out[...] = row_factor[0:1]
    row_inv = lax.dot_general(
        1.0 / row_factor, ones * 0.125, (((0,), (0,)), ((), ())), precision=HI,
        preferred_element_type=F32,
    )

    def weighted(i, carry):
        g = grad[:, aligned(i * 256, 256, 256)]
        sums = jnp.sum(g * g * row_inv[:, 0:1], axis=0, keepdims=True)
        for j in range(2):
            block = i * 2 + j
            vec[lax.div(block, 3), pl.ds(3 + lax.rem(block, 3), 1), :] = (
                sums[:, j * 128:(j + 1) * 128]
            )
        return carry

    lax.fori_loop(0, COLS // 256, weighted, 0)

    sum_in = [
        remote(vec.at[rot(dp, k, NZ)], vec_z.at[k], zdev(k)) for k in range(1, NZ)
    ]
    total = vec[dp]
    for k in range(1, NZ):
        sum_in[k - 1].wait_recv()
        total = total + vec_z[k]
    vec_xy[0] = total
    sum_in = [
        remote(vec_xy.at[0], vec_xy.at[k], pdev(k)) for k in range(1, PLANE)
    ]
    old = []
    for d in range(4):
        base = rot(mc, -d, 4) * 24 + dp * 3
        old.append(jnp.concatenate(
            [col_old[pl.ds(base + j, 1), :] for j in range(3)], axis=0
        ))
    totals = [total, None, None, None]
    for k in range(1, PLANE):
        sum_in[k - 1].wait_recv()
    for k in range(1, PLANE):
        d = k % 4
        totals[d] = vec_xy[k] if totals[d] is None else totals[d] + vec_xy[k]
    square = jnp.zeros((3, 128), F32)
    moved = jnp.zeros((3, 128), F32)
    col_part = []
    for d in range(4):
        col_part.append(SECOND_DECAY * old[d] + (1.0 - SECOND_DECAY) * (
            totals[d][0:3] * (1.0 / D) + SQUARE_EPS
        ))
        square = square + totals[d][0:3]
        moved = moved + totals[d][3:6] / col_part[d]
    w_total = ((totals[0] + totals[1]) + totals[2]) + totals[3]
    scal[...] = jnp.zeros((8, 128), F32)
    scal[0:3] = col_part[0]
    scal[3:4] = jnp.sum(square, axis=0, keepdims=True)
    scal[4:5] = jnp.sum(moved, axis=0, keepdims=True)
    sum_in = [
        remote(scal, col_all.at[dp], zdev(k)) for k in range(1, NZ)
    ]
    col_all[dp] = scal[...]
    old_total = jnp.sum(row_old[...])
    row_root = jnp.sqrt(row_inv)
    for copy in sum_in:
        copy.wait_recv()
    sums = col_all[0]
    for k in range(1, NZ):
        sums = sums + col_all[k]
    for k in range(NZ):
        for j in range(3):
            cols = slice((k * 3 + j) * 128, (k * 3 + j + 1) * 128)
            cf_out[:, cols] = col_all[k, j:j + 1, :]
    cs_buf[...] = lax.rsqrt(cf_out[...])
    square_total = jnp.sum(sums[3:4], axis=1, keepdims=True)
    moved_total = jnp.sum(sums[4:5], axis=1, keepdims=True)
    row_mean = (
        SECOND_DECAY * old_total
        + (1.0 - SECOND_DECAY) * (square_total * (1.0 / QW) + D * SQUARE_EPS)
    ) * (1.0 / D)
    entries = float(D) * float(QW)
    clip = jnp.maximum(1.0, jnp.sqrt(row_mean * moved_total * (1.0 / entries)))
    w_scale = jnp.sqrt(w_total[6:7, 0:1] * (1.0 / entries))
    rs_buf[...] = row_root * (w_scale * jnp.sqrt(row_mean) / clip)

    w_in = []
    for c in range(NCHUNK):
        def update(i, carry, c=c):
            cols = aligned(STARTS[c] + i * 256, 256, 256)
            step = grad[:, cols] * (rs_buf[:, 0:1] * cs_buf[0:1, cols])
            new_w = w_buf[:, cols] - STEP_RATE * step
            grad[:, cols] = step
            w_buf[:, cols] = new_w
            w_own[:, cols] = new_w.astype(BF16)
            return carry

        lax.fori_loop(0, WIDTHS[c] // 256, update, 0)
        cols = pl.ds(STARTS[c], WIDTHS[c])
        w_in.append(remote(w_own.at[:, cols], w_peer.at[:, cols], ymate))
    outs = [
        pltpu.make_async_copy(w_buf, w_out, local_sem.at[4]),
        pltpu.make_async_copy(grad, s_out, local_sem.at[5]),
    ]
    for copy in outs:
        copy.start()
    nxt_fwd = []
    for j in range(2):
        for k in range(1, NZ):
            nxt_in[j, k].wait_recv()
        ref = nxt_all.at[j, :, aligned(core * q_rows, q_rows, 16)]
        nxt_fwd.append(remote(ref, ref, sib))
    for copy in nxt_fwd:
        copy.wait_recv()

    opp_in = {}
    q_in = {}
    z_part = {}
    x_next = rot(x, 1, NX)
    x_prev = rot(x, 3, NX)
    x_opp = rot(x, 2, NX)

    def block(c, q, lo, hi):
        return part[c % SLOTS, :, q, :, lo:hi].reshape(NZ * QTOK, hi - lo)

    def stage_matmul(c):
        w_in[c].wait_recv()
        width = WIDTHS[c]
        hw = width // 2

        def one(i, carry):
            src = aligned(STARTS[c] + i * 256, 256, 256)
            for r in range(2):
                zs = slice(r * 4, (r + 1) * 4)
                p = jnp.dot(
                    nxt_all[0, zs].reshape(4 * HALF, FEAT), w_own[:, src],
                    preferred_element_type=F32,
                )
                p = p + jnp.dot(
                    nxt_all[1, zs].reshape(4 * HALF, FEAT), w_peer[:, src],
                    preferred_element_type=F32,
                )
                part[c % SLOTS, zs, :, :, aligned(i * 256, 256, 256)] = (
                    p.reshape(4, NX, QTOK, 256)
                )
            return carry

        lax.fori_loop(0, width // 256, one, 0)
        cols = pl.ds(STARTS[c] // 2, hw)
        for j, sign in ((0, 1), (1, -1)):
            opp_send[j, :, cols] = block(c, x_opp, j * hw, (j + 1) * hw).astype(BF16)
            opp_in[c, j] = remote(
                opp_send.at[j, :, cols], opp_recv.at[j, :, cols], xdev(sign)
            )

    def stage_relay(c):
        width = WIDTHS[c]
        hw = width // 2
        base = STARTS[c]
        cols = pl.ds(base // 2, hw)
        for j, sign, q in ((0, 1, x_next), (1, -1, x_prev)):
            opp_in[c, j].wait_recv()
            lo = j * hw
            x_send[j, :, base + lo:base + lo + hw] = (
                block(c, q, lo, lo + hw) + opp_recv[j, :, cols].astype(F32)
            ).astype(BF16)
            lo = hw - lo
            x_send[j, :, base + lo:base + lo + hw] = block(c, q, lo, lo + hw).astype(BF16)
            full = pl.ds(base, width)
            q_in[c, j] = remote(x_send.at[j, :, full], x_recv.at[j, :, full], xdev(sign))

    def stage_z(c):
        width = WIDTHS[c]
        hw = width // 2
        base = STARTS[c]
        q_in[c, 0].wait_recv()
        q_in[c, 1].wait_recv()
        full = slice(base, base + width)
        summed = (
            block(c, x, 0, width)
            + x_recv[0, :, full].astype(F32) + x_recv[1, :, full].astype(F32)
        ).reshape(NZ, QTOK, width)
        part[c % SLOTS, :, x, :, 0:width] = summed
        cols = pl.ds(base // 2, hw)
        z_send[:, :, cols] = jnp.concatenate(
            [summed[:, :, :hw], summed[:, :, hw:]], axis=1
        ).astype(BF16)
        for k in range(1, NZ):
            z_part[c, k] = remote(
                z_send.at[rot(dp, k, NZ), :, cols], z_recv.at[k, :, cols], zdev(k)
            )
        q_out[:, full] = part[c % SLOTS, dp, x, :, 0:width]

    def stage_out(c):
        hw = WIDTHS[c] // 2
        acc = None
        for k in range(1, NZ):
            z_part[c, k].wait_recv()
            term = z_recv[k, :, pl.ds(STARTS[c] // 2, hw)].astype(F32)
            acc = term if acc is None else acc + term
        for j in range(2):
            cols = pl.ds(STARTS[c] + j * hw, hw)
            q_out[:, cols] = (q_out[:, cols] + acc[j * QTOK:(j + 1) * QTOK]) * D ** (-0.5)

    for t in range(NCHUNK):
        stage_matmul(t)
        if t >= 1:
            stage_relay(t - 1)
        if t >= 3:
            stage_z(t - 3)
        if t >= 5:
            stage_out(t - 5)
    stage_relay(NCHUNK - 1)
    for t in range(NCHUNK - 3, NCHUNK):
        stage_z(t)
    for t in range(NCHUNK - 5, NCHUNK):
        stage_out(t)

    for copy in outs:
        copy.wait()
    for copy in sent:
        copy.wait_send()
    assert count[0] <= N_SEM


def finish(*refs):
    src, dst, buf, sem = refs[:5], refs[5:10], refs[10:15], refs[15]
    views = []
    for i in range(2):
        for r in range(6):
            views.append((i, pl.ds(r * 48, 48)))
    views += [(i, slice(None)) for i in range(2, 5)]
    into = [
        pltpu.make_async_copy(src[i].at[rows], buf[i].at[rows], sem.at[0, n])
        for n, (i, rows) in enumerate(views)
    ]
    out = [
        pltpu.make_async_copy(buf[i].at[rows], dst[i].at[rows], sem.at[1, n])
        for n, (i, rows) in enumerate(views)
    ]
    for copy in into:
        copy.start()
    for first, second in zip(into, out):
        first.wait()
        second.start()
    for copy in out:
        copy.wait()


def body(weight, activations, cotangent, row_old, col_old, next_input):
    vm = pl.BlockSpec(memory_space=pltpu.VMEM)
    hbm = pl.BlockSpec(memory_space=pl.ANY)
    v = pltpu.VMEM

    def shape(*dims):
        return jax.ShapeDtypeStruct(dims, F32)

    new_weight, scaled_step, queries, row_factor, col_factor = pl.pallas_call(
        kernel,
        out_shape=(
            shape(FEAT, COLS), shape(FEAT, COLS), shape(QTOK, COLS), shape(1, FEAT),
            shape(1, COLS),
        ),
        in_specs=[hbm, hbm, hbm, hbm, vm, vm],
        out_specs=(hbm, hbm, vm, vm, vm),
        scratch_shapes=[
            v((FEAT, 128), F32),
            v((1, COLS), F32),
            v((TOKENS, COLS), BF16),
            v((FEAT, COLS), F32),
            v((FEAT, COLS), F32),
            v((TOK, BLOCK), BF16),
            v((NZ, TOK, FEAT), BF16),
            v((TOKENS, FEAT), BF16),
            v((FEAT, TOKENS), BF16),
            v((TOK, BLOCK), BF16),
            v((NZ, TOK, FEAT), BF16),
            v((NZ, HALF // 2, FEAT), BF16),
            v((2, NZ, HALF, FEAT), BF16),
            v((FEAT, 128), F32),
            v((8, FEAT), F32),
            v((4, 8, FEAT), F32),
            v((NZ, 8, 128), F32),
            v((NZ, 8, 128), F32),
            v((PLANE, 8, 128), F32),
            v((NZ, 8, 128), F32),
            v((8, 128), F32),
            v((FEAT, COLS), BF16),
            v((FEAT, COLS), BF16),
            v((SLOTS, NZ, NX, QTOK, WMAX), F32),
            v((2, TOK, COLS // 2), BF16),
            v((2, TOK, COLS // 2), BF16),
            v((2, TOK, COLS), BF16),
            v((2, TOK, COLS), BF16),
            v((NZ, 2 * QTOK, COLS // 2), BF16),
            v((NZ, 2 * QTOK, COLS // 2), BF16),
            pltpu.SemaphoreType.DMA((6,)),
            pltpu.SemaphoreType.DMA((N_SEM,)),
            pltpu.SemaphoreType.DMA((N_SEM,)),
        ],
        compiler_params=pltpu.CompilerParams(
            collective_id=0, has_side_effects=True, vmem_limit_bytes=60 * 1024 * 1024
        ),
        cost_estimate=pl.CostEstimate(
            flops=4 * TOKENS * FEAT * COLS, bytes_accessed=16_000_000, transcendentals=0
        ),
        name="update",
    )(
        cotangent, activations, next_input, weight,
        row_old.reshape(D // 128, 128), col_old.reshape(QW // 128, 128),
    )
    shapes = (
        shape(FEAT, COLS), shape(FEAT, COLS), shape(QTOK, COLS), shape(1, FEAT),
        shape(1, COLS),
    )
    new_weight, scaled_step, queries, row_factor, col_factor = pl.pallas_call(
        finish,
        in_specs=[hbm] * 5,
        out_specs=(hbm,) * 5,
        out_shape=shapes,
        scratch_shapes=[*(v(a.shape, F32) for a in shapes), pltpu.SemaphoreType.DMA((2, 15))],
        compiler_params=pltpu.CompilerParams(vmem_limit_bytes=60 * 1024 * 1024),
        cost_estimate=pl.CostEstimate(
            flops=0, bytes_accessed=16 * FEAT * COLS, transcendentals=0
        ),
        name="finish",
    )(new_weight, scaled_step, queries, row_factor, col_factor)
    return (
        new_weight, row_factor.reshape(FEAT), col_factor.reshape(COLS), queries, scaled_step,
    )


def solution(mesh):
    placed = (
        P(("mrow", "dp"), "mcol"),
        P("dp", "mrow"),
        P("dp", "mcol"),
        P(),
        P(),
        P("dp", "mrow"),
    )
    return jax.shard_map(
        body,
        mesh=mesh,
        in_specs=placed,
        out_specs=(
            P(("mrow", "dp"), "mcol"),
            P(("mrow", "dp")),
            P("mcol"),
            P(("dp", "mrow"), "mcol"),
            P(("mrow", "dp"), "mcol"),
        ),
        check_vma=False,
    )
```

```python
import jax
import jax.numpy as jnp
from jax import lax
from jax.experimental import pallas as pl
from jax.experimental.pallas import tpu as pltpu
from jax.sharding import PartitionSpec as P

SECOND_DECAY = 1.0 - 10.0 ** (-0.8)
SQUARE_EPS = 1e-30
STEP_RATE = 0.01

NZ = 8
NX = 4
PLANE = 32
TOK = 192
D = 18432
QW = 12288
TOKENS = 1536
FEAT = 288
BLOCK = 2304
COLS = 3072
HALF = 96
QTOK = 24
B_COLS = 128
E_BASE = 512
E_COLS = 768
H_BASE = 2048
H_COLS = 256
WIDTHS = (256,) * 12
STARTS = tuple(sum(WIDTHS[:i]) for i in range(len(WIDTHS)))
NCHUNK = len(WIDTHS)
WMAX = max(WIDTHS)
SLOTS = 4
N_SEM = 384
MESH = pl.DeviceIdType.MESH
HI = lax.Precision.HIGHEST
F32 = jnp.float32
BF16 = jnp.bfloat16


def rot(base, step, size):
    return lax.rem(base + (step + size) % size, size)


def aligned(start, size, mult):
    return pl.ds(pl.multiple_of(start, mult), size)


def kernel(
    cot_hbm, act_hbm, nxt_hbm, w_hbm, row_old, col_old,
    w_out, s_out, q_out, rf_out, cf_out,
    rs_buf, cs_buf, cot, grad, w_buf, act, act_s, act_all, act_t, nxt, nxt_s, nxt_y, nxt_all,
    row_acc, row_send, row_recv, vec, vec_z, vec_xy, col_all, scal,
    w_own, w_peer, part, opp_send, opp_recv, x_send, x_recv, z_send, z_recv,
    local_sem, send_sem, recv_sem,
):
    dp = lax.axis_index("dp")
    mr = lax.axis_index("mrow")
    mc = lax.axis_index("mcol")
    x = lax.rem(mr, NX)
    y = lax.div(mr, NX)
    core = lax.rem(mc, 2)
    sib = {"mcol": mc + 1 - 2 * core}
    ymate = {"mrow": (1 - y) * NX + x}
    count = [0]
    sent = []

    def remote(src, dst, dev):
        i = count[0]
        count[0] += 1
        copy = pltpu.make_async_remote_copy(
            src_ref=src, dst_ref=dst, send_sem=send_sem.at[i], recv_sem=recv_sem.at[i],
            device_id=dev, device_id_type=MESH,
        )
        copy.start()
        sent.append(copy)
        return copy

    def zdev(k):
        return {"dp": rot(dp, k, NZ)}

    def pdev(k):
        place = rot(mr * 4 + mc, k, PLANE)
        return {"mrow": lax.div(place, 4), "mcol": lax.rem(place, 4)}

    def xdev(k):
        return {"mrow": y * NX + rot(x, k, NX)}

    def zrows(k, half=None):
        if half is None:
            return aligned(rot(dp, k, NZ) * TOK, TOK, 64)
        return aligned(rot(dp, k, NZ) * TOK + half * HALF, HALF, 32)

    loads = [
        pltpu.make_async_copy(act_hbm, act, local_sem.at[0]),
        pltpu.make_async_copy(cot_hbm, cot.at[zrows(0)], local_sem.at[1]),
        pltpu.make_async_copy(nxt_hbm, nxt, local_sem.at[2]),
        pltpu.make_async_copy(w_hbm, w_buf, local_sem.at[3]),
    ]
    for load in loads:
        load.start()

    barrier = pltpu.get_barrier_semaphore()
    for k in range(1, NZ):
        pl.semaphore_signal(barrier, inc=1, device_id=zdev(k), device_id_type=MESH)
    for k in range(1, PLANE):
        pl.semaphore_signal(barrier, inc=1, device_id=pdev(k), device_id_type=MESH)
    loads[0].wait()
    for k in range(NZ):
        act_s[k] = act[:, k * FEAT:(k + 1) * FEAT]
    loads[1].wait()
    loads[2].wait()
    for k in range(NZ):
        nxt_s[k] = nxt[:, k * FEAT:(k + 1) * FEAT]
    pl.semaphore_wait(barrier, NZ + PLANE - 2)

    even = lax.rem(x, 2)
    flows = {
        "h": (H_BASE + (2 * y + even) * H_COLS, H_COLS),
        "b": (x * B_COLS, B_COLS),
        "e": (E_BASE + even * E_COLS, E_COLS // 2),
        "f": (E_BASE + even * E_COLS + E_COLS // 2, E_COLS // 2),
    }
    moves = {"h": (1 - 2 * even) * H_COLS, "e": (1 - 2 * even) * E_COLS}
    moves["f"] = moves["e"]
    z_in = {}

    def z_step(f, s):
        start, width = flows[f]
        cols = aligned(start, width, 128)
        for sign in (1, -1):
            half = None if s < 4 else (1 - sign) // 2
            ref = cot.at[zrows(-sign * (s - 1), half), cols]
            z_in[f, sign, s] = remote(ref, ref, zdev(sign))

    def z_next(f, s):
        for sign in (1, -1):
            z_in[f, sign, s].wait_recv()
        if s < 4:
            z_step(f, s + 1)

    def pieces(s):
        return (4,) if s == 4 else (-s, s)

    x_in = {}
    b_in = {}
    y_in = {}

    def x_ref(k, f, half):
        start, width = flows[f]
        return cot.at[zrows(k, half), aligned(start, width, 128)]

    def x_send_pair(f, k):
        for sign in (1, -1):
            ref = x_ref(k, f, (1 - sign) // 2)
            x_in[f, k, sign] = remote(ref, ref, xdev(sign))

    def b_direct(k):
        for sign in (1, -1):
            ref = x_ref(k, "b", None)
            x_in["b", k, sign] = remote(ref, ref, xdev(sign))

    def b_forward(k):
        for sign in (1, -1):
            x_in["b", k, sign].wait_recv()
            ref = cot.at[
                zrows(k, (1 - sign) // 2), aligned(rot(x, -sign, NX) * B_COLS, B_COLS, 128)
            ]
            b_in[k, sign] = remote(ref, ref, xdev(sign))

    def y_own(k):
        ref = x_ref(k, "h", None)
        y_in[k, 0] = remote(ref, ref, ymate)

    def y_other(k):
        for sign in (1, -1):
            x_in["h", k, sign].wait_recv()
        ref = cot.at[zrows(k), aligned(flows["h"][0] + moves["h"], H_COLS, 128)]
        y_in[k, 1] = remote(ref, ref, ymate)

    quarter = core * HALF + lax.div(mc, 2) * (HALF // 2)
    act_in = {}
    act_mid = {}
    act_fwd = {}

    def act_rows(k):
        return aligned(rot(dp, k, NZ) * TOK + quarter, HALF // 2, 16)

    def act_send(k):
        act_in[k] = remote(
            act_s.at[rot(dp, k, NZ), aligned(quarter, HALF // 2, 16)],
            act_all.at[act_rows(0)], zdev(k),
        )

    def act_middle(k):
        act_in[k].wait_recv()
        ref = act_all.at[act_rows(-k)]
        act_mid[k] = remote(ref, ref, {"mcol": rot(mc, 2, 4)})

    def act_forward(k):
        act_mid[k].wait_recv()
        ref = act_all.at[zrows(-k, core)]
        act_fwd[k] = remote(ref, ref, sib)

    for f in ("h", "b", "e", "f"):
        z_step(f, 1)
    for s in range(1, 5):
        z_next("h", s)
        for k in pieces(s):
            x_send_pair("h", k)
            y_own(k)
        z_next("b", s)
        for k in pieces(s):
            b_direct(k)
        if s == 1:
            for k in (4, 3, 5):
                act_send(k)
            act_all[zrows(0), :] = act_s[dp]
            loads[3].wait()

            def weight_square(i, total):
                tile = w_buf[:, aligned(i * 256, 256, 256)]
                return total + jnp.sum((tile * tile).reshape(FEAT // 8, 8, 256), axis=0)

            wsq = lax.fori_loop(0, COLS // 256, weight_square, jnp.zeros((8, 256), F32))
            vec[...] = jnp.zeros((NZ, 8, 128), F32) + jnp.sum(wsq)
            row_acc[...] = jnp.zeros((FEAT, 128), F32)
        if s == 2:
            for k in (2, 6, 1, 7):
                act_send(k)
        if s > 1:
            for k in pieces(s - 1):
                y_other(k)
                b_forward(k)
        if s == 2:
            for k in (4, 3, 5):
                act_middle(k)
        if s == 3:
            for k in (2, 6, 1, 7):
                act_middle(k)
        if s == 4:
            for k in (4, 3, 5, 2, 6, 1, 7):
                act_forward(k)
        for f in ("e", "f"):
            z_next(f, s)
            for k in pieces(s):
                x_send_pair(f, k)

    q_rows = HALF // 2

    def nxt_part(z, j):
        return nxt_all.at[j, z, aligned(core * q_rows, q_rows, 16)]

    mine = aligned(y * HALF + core * q_rows, q_rows, 16)
    nxt_in = {}

    def nxt_send(j):
        for k in range(1, NZ):
            src = nxt_s.at[rot(dp, k, NZ), mine] if j == 0 else nxt_y.at[rot(dp, k, NZ)]
            nxt_in[j, k] = remote(src, nxt_part(dp, j), zdev(k))
        nxt_part(dp, j)[...] = nxt_s[dp, mine, :] if j == 0 else nxt_y[dp]

    y_other(4)
    b_forward(4)
    nxt_send(0)
    nxt_mate = remote(
        nxt_s.at[:, aligned((1 - y) * HALF + core * q_rows, q_rows, 16)], nxt_y, ymate
    )
    for k in range(1, NZ):
        act_fwd[k].wait_recv()
    for i in range(4):
        rows = slice(i * 384, (i + 1) * 384)
        act_t[:, rows] = act_all[rows, :].T

    def grad_tiles(base, tiles):
        def one(i, carry):
            start = base + i * 256
            cols = aligned(start, 256, 256)
            g = jnp.dot(act_t[...], cot[:, cols], preferred_element_type=F32)
            grad[:, cols] = g
            sq = g * g
            row_acc[...] += sq[:, :128] + sq[:, 128:]
            sums = jnp.sum(sq, axis=0, keepdims=True)
            for j in range(2):
                block = lax.div(start, 128) + j
                vec[lax.div(block, 3), pl.ds(lax.rem(block, 3), 1), :] = (
                    sums[:, j * 128:(j + 1) * 128]
                )
            return carry

        lax.fori_loop(0, tiles, one, 0)

    every = (-1, 1, -2, 2, -3, 3, 4)
    grad_tiles(H_BASE + y * 2 * H_COLS, 2 * H_COLS // 256)
    for k in every:
        for sign in (1, -1):
            b_in[k, sign].wait_recv()
    grad_tiles(0, NX * B_COLS // 256)
    grad_tiles(flows["e"][0], E_COLS // 256)
    for k in every:
        for j in range(2):
            y_in[k, j].wait_recv()
    grad_tiles(H_BASE + (1 - y) * 2 * H_COLS, 2 * H_COLS // 256)
    for k in every:
        for sign in (1, -1):
            x_in["e", k, sign].wait_recv()
            x_in["f", k, sign].wait_recv()
    grad_tiles(flows["e"][0] + moves["e"], E_COLS // 256)

    ones = jnp.ones((8, 128), F32)
    row_send[...] = lax.dot_general(
        ones, row_acc[...], (((1,), (1,)), ((), ())), precision=HI, preferred_element_type=F32
    )
    row_in = [
        remote(row_send, row_recv.at[k], {"mcol": rot(mc, k, 4)}) for k in range(1, 4)
    ]
    place = (mr * NZ + dp) * (FEAT // 32)
    first = lax.div(place, 4)
    shift = lax.rem(place, 4)
    near = jnp.concatenate([row_old[pl.ds(first + j, 1), :] for j in range(3)], axis=1)
    row_mine = near[:, 0:FEAT]
    for j in range(1, 4):
        row_mine = jnp.where(shift == j, near[:, j * 32:j * 32 + FEAT], row_mine)
    for copy in row_in:
        copy.wait_recv()
    row_full = ((row_send[...] + row_recv[1]) + row_recv[2]) + row_recv[3]
    row_factor = SECOND_DECAY * row_mine + (1.0 - SECOND_DECAY) * (
        row_full * (1.0 / QW) + SQUARE_EPS
    )
    rf_out[...] = row_factor[0]
    row_inv = lax.dot_general(
        1.0 / row_factor, ones * 0.125, (((0,), (0,)), ((), ())), precision=HI,
        preferred_element_type=F32,
    )

    def weighted(i, carry):
        for j in range(2):
            block = i * 2 + j
            g = grad[:, aligned(block * 128, 128, 128)]
            vec[lax.div(block, 3), pl.ds(3 + lax.rem(block, 3), 1), :] = (
                jnp.sum(g * g * row_inv, axis=0, keepdims=True)
            )
        return carry

    lax.fori_loop(0, COLS // 256, weighted, 0)

    sum_in = [
        remote(vec.at[rot(dp, k, NZ)], vec_z.at[k], zdev(k)) for k in range(1, NZ)
    ]
    total = vec[dp]
    for k in range(1, NZ):
        sum_in[k - 1].wait_recv()
        total = total + vec_z[k]
    vec_xy[0] = total
    sum_in = [
        remote(vec_xy.at[0], vec_xy.at[k], pdev(k)) for k in range(1, PLANE)
    ]
    old = []
    for d in range(4):
        base = rot(mc, -d, 4) * 24 + dp * 3
        old.append(jnp.concatenate(
            [col_old[pl.ds(base + j, 1), :] for j in range(3)], axis=0
        ))
    totals = [total, None, None, None]
    for k in range(1, PLANE):
        sum_in[k - 1].wait_recv()
    for k in range(1, PLANE):
        d = k % 4
        totals[d] = vec_xy[k] if totals[d] is None else totals[d] + vec_xy[k]
    square = jnp.zeros((3, 128), F32)
    moved = jnp.zeros((3, 128), F32)
    col_part = []
    for d in range(4):
        col_part.append(SECOND_DECAY * old[d] + (1.0 - SECOND_DECAY) * (
            totals[d][0:3] * (1.0 / D) + SQUARE_EPS
        ))
        square = square + totals[d][0:3]
        moved = moved + totals[d][3:6] / col_part[d]
    w_total = ((totals[0] + totals[1]) + totals[2]) + totals[3]
    scal[...] = jnp.zeros((8, 128), F32)
    scal[0:3] = col_part[0]
    scal[3:4] = jnp.sum(square, axis=0, keepdims=True)
    scal[4:5] = jnp.sum(moved, axis=0, keepdims=True)
    sum_in = [
        remote(scal, col_all.at[dp], zdev(k)) for k in range(1, NZ)
    ]
    col_all[dp] = scal[...]
    nxt_mate.wait_recv()
    nxt_send(1)
    old_total = jnp.sum(row_old[...])
    row_root = jnp.sqrt(row_inv)
    for copy in sum_in:
        copy.wait_recv()
    sums = col_all[0]
    for k in range(1, NZ):
        sums = sums + col_all[k]
    for k in range(NZ):
        for j in range(3):
            cols = slice((k * 3 + j) * 128, (k * 3 + j + 1) * 128)
            cf_out[:, cols] = col_all[k, j:j + 1, :]
    cs_buf[...] = lax.rsqrt(cf_out[...])
    square_total = jnp.sum(sums[3:4], axis=1, keepdims=True)
    moved_total = jnp.sum(sums[4:5], axis=1, keepdims=True)
    row_mean = (
        SECOND_DECAY * old_total
        + (1.0 - SECOND_DECAY) * (square_total * (1.0 / QW) + D * SQUARE_EPS)
    ) * (1.0 / D)
    entries = float(D) * float(QW)
    clip = jnp.maximum(1.0, jnp.sqrt(row_mean * moved_total * (1.0 / entries)))
    w_scale = jnp.sqrt(w_total[6:7, 0:1] * (1.0 / entries))
    rs_buf[...] = row_root * (w_scale * jnp.sqrt(row_mean) / clip)

    w_in = []
    for c in range(NCHUNK):
        def update(i, carry, c=c):
            cols = aligned(STARTS[c] + i * 128, 128, 128)
            step = grad[:, cols] * (rs_buf[...] * cs_buf[0:1, cols])
            new_w = w_buf[:, cols] - STEP_RATE * step
            grad[:, cols] = step
            w_buf[:, cols] = new_w
            w_own[:, cols] = new_w.astype(BF16)
            return carry

        lax.fori_loop(0, WIDTHS[c] // 128, update, 0)
        cols = pl.ds(STARTS[c], WIDTHS[c])
        w_in.append(remote(w_own.at[:, cols], w_peer.at[:, cols], ymate))
    outs = [
        pltpu.make_async_copy(w_buf, w_out, local_sem.at[4]),
        pltpu.make_async_copy(grad, s_out, local_sem.at[5]),
    ]
    for copy in outs:
        copy.start()
    nxt_fwd = []
    for j in range(2):
        for k in range(1, NZ):
            nxt_in[j, k].wait_recv()
        ref = nxt_all.at[j, :, aligned(core * q_rows, q_rows, 16)]
        nxt_fwd.append(remote(ref, ref, sib))
    for copy in nxt_fwd:
        copy.wait_recv()

    opp_in = {}
    q_in = {}
    z_part = {}
    x_next = rot(x, 1, NX)
    x_prev = rot(x, 3, NX)
    x_opp = rot(x, 2, NX)

    def block(c, q, lo, hi):
        return part[c % SLOTS, :, q, :, lo:hi].reshape(NZ * QTOK, hi - lo)

    def stage_matmul(c):
        w_in[c].wait_recv()
        width = WIDTHS[c]
        hw = width // 2

        def one(i, carry):
            src = aligned(STARTS[c] + i * 256, 256, 256)
            for r in range(2):
                zs = slice(r * 4, (r + 1) * 4)
                p = jnp.dot(
                    nxt_all[0, zs].reshape(4 * HALF, FEAT), w_own[:, src],
                    preferred_element_type=F32,
                )
                p = p + jnp.dot(
                    nxt_all[1, zs].reshape(4 * HALF, FEAT), w_peer[:, src],
                    preferred_element_type=F32,
                )
                part[c % SLOTS, zs, :, :, aligned(i * 256, 256, 256)] = (
                    p.reshape(4, NX, QTOK, 256)
                )
            return carry

        lax.fori_loop(0, width // 256, one, 0)
        cols = pl.ds(STARTS[c] // 2, hw)
        for j, sign in ((0, 1), (1, -1)):
            opp_send[j, :, cols] = block(c, x_opp, j * hw, (j + 1) * hw).astype(BF16)
            opp_in[c, j] = remote(
                opp_send.at[j, :, cols], opp_recv.at[j, :, cols],
                xdev(sign),
            )

    def stage_relay(c):
        width = WIDTHS[c]
        hw = width // 2
        base = STARTS[c]
        cols = pl.ds(base // 2, hw)
        for j, sign, q in ((0, 1, x_next), (1, -1, x_prev)):
            opp_in[c, j].wait_recv()
            lo = j * hw
            x_send[j, :, base + lo:base + lo + hw] = (
                block(c, q, lo, lo + hw) + opp_recv[j, :, cols].astype(F32)
            ).astype(BF16)
            lo = hw - lo
            x_send[j, :, base + lo:base + lo + hw] = block(c, q, lo, lo + hw).astype(BF16)
            full = pl.ds(base, width)
            q_in[c, j] = remote(x_send.at[j, :, full], x_recv.at[j, :, full], xdev(sign))

    def stage_z(c):
        width = WIDTHS[c]
        hw = width // 2
        base = STARTS[c]
        q_in[c, 0].wait_recv()
        q_in[c, 1].wait_recv()
        full = slice(base, base + width)
        summed = (
            block(c, x, 0, width)
            + x_recv[0, :, full].astype(F32) + x_recv[1, :, full].astype(F32)
        ).reshape(NZ, QTOK, width)
        part[c % SLOTS, :, x, :, 0:width] = summed
        cols = pl.ds(base // 2, hw)
        z_send[:, :, cols] = jnp.concatenate(
            [summed[:, :, :hw], summed[:, :, hw:]], axis=1
        ).astype(BF16)
        for k in range(1, NZ):
            z_part[c, k] = remote(
                z_send.at[rot(dp, k, NZ), :, cols], z_recv.at[k, :, cols], zdev(k)
            )
        q_out[:, full] = part[c % SLOTS, dp, x, :, 0:width]

    def stage_out(c):
        hw = WIDTHS[c] // 2
        acc = None
        for k in range(1, NZ):
            z_part[c, k].wait_recv()
            term = z_recv[k, :, pl.ds(STARTS[c] // 2, hw)].astype(F32)
            acc = term if acc is None else acc + term
        for j in range(2):
            cols = pl.ds(STARTS[c] + j * hw, hw)
            q_out[:, cols] = (q_out[:, cols] + acc[j * QTOK:(j + 1) * QTOK]) * D ** (-0.5)

    for t in range(NCHUNK):
        stage_matmul(t)
        if t >= 1:
            stage_relay(t - 1)
        if t >= 3:
            stage_z(t - 3)
        if t >= 5:
            stage_out(t - 5)
    stage_relay(NCHUNK - 1)
    for t in range(NCHUNK - 3, NCHUNK):
        stage_z(t)
    for t in range(NCHUNK - 5, NCHUNK):
        stage_out(t)

    for copy in outs:
        copy.wait()
    for copy in sent:
        copy.wait_send()
    assert count[0] <= N_SEM


def finish(*refs):
    src, dst, buf, sem = refs[:5], refs[5:10], refs[10:15], refs[15]
    views = []
    for i in range(2):
        for r in range(6):
            views.append((i, pl.ds(r * 48, 48)))
    views += [(i, slice(None)) for i in range(2, 5)]
    into = [
        pltpu.make_async_copy(src[i].at[rows], buf[i].at[rows], sem.at[0, n])
        for n, (i, rows) in enumerate(views)
    ]
    out = [
        pltpu.make_async_copy(buf[i].at[rows], dst[i].at[rows], sem.at[1, n])
        for n, (i, rows) in enumerate(views)
    ]
    for copy in into:
        copy.start()
    for first, second in zip(into, out):
        first.wait()
        second.start()
    for copy in out:
        copy.wait()


def body(weight, activations, cotangent, row_old, col_old, next_input):
    vm = pl.BlockSpec(memory_space=pltpu.VMEM)
    hbm = pl.BlockSpec(memory_space=pl.ANY)
    v = pltpu.VMEM

    def shape(*dims):
        return jax.ShapeDtypeStruct(dims, F32)

    new_weight, scaled_step, queries, row_factor, col_factor = pl.pallas_call(
        kernel,
        out_shape=(
            shape(FEAT, COLS), shape(FEAT, COLS), shape(QTOK, COLS), shape(FEAT),
            shape(1, COLS),
        ),
        in_specs=[hbm, hbm, hbm, hbm, vm, vm],
        out_specs=(hbm, hbm, vm, vm, vm),
        scratch_shapes=[
            v((FEAT, 128), F32),
            v((1, COLS), F32),
            v((TOKENS, COLS), BF16),
            v((FEAT, COLS), F32),
            v((FEAT, COLS), F32),
            v((TOK, BLOCK), BF16),
            v((NZ, TOK, FEAT), BF16),
            v((TOKENS, FEAT), BF16),
            v((FEAT, TOKENS), BF16),
            v((TOK, BLOCK), BF16),
            v((NZ, TOK, FEAT), BF16),
            v((NZ, HALF // 2, FEAT), BF16),
            v((2, NZ, HALF, FEAT), BF16),
            v((FEAT, 128), F32),
            v((8, FEAT), F32),
            v((4, 8, FEAT), F32),
            v((NZ, 8, 128), F32),
            v((NZ, 8, 128), F32),
            v((PLANE, 8, 128), F32),
            v((NZ, 8, 128), F32),
            v((8, 128), F32),
            v((FEAT, COLS), BF16),
            v((FEAT, COLS), BF16),
            v((SLOTS, NZ, NX, QTOK, WMAX), F32),
            v((2, TOK, COLS // 2), BF16),
            v((2, TOK, COLS // 2), BF16),
            v((2, TOK, COLS), BF16),
            v((2, TOK, COLS), BF16),
            v((NZ, 2 * QTOK, COLS // 2), BF16),
            v((NZ, 2 * QTOK, COLS // 2), BF16),
            pltpu.SemaphoreType.DMA((6,)),
            pltpu.SemaphoreType.DMA((N_SEM,)),
            pltpu.SemaphoreType.DMA((N_SEM,)),
        ],
        compiler_params=pltpu.CompilerParams(
            collective_id=0, has_side_effects=True, vmem_limit_bytes=60 * 1024 * 1024
        ),
        cost_estimate=pl.CostEstimate(
            flops=4 * TOKENS * FEAT * COLS, bytes_accessed=16_000_000, transcendentals=0
        ),
        name="update",
    )(
        cotangent, activations, next_input, weight,
        row_old.reshape(D // 128, 128), col_old.reshape(QW // 128, 128),
    )
    shapes = (
        shape(FEAT, COLS), shape(FEAT, COLS), shape(QTOK, COLS), shape(FEAT),
        shape(1, COLS),
    )
    new_weight, scaled_step, queries, row_factor, col_factor = pl.pallas_call(
        finish,
        in_specs=[hbm] * 5,
        out_specs=(hbm,) * 5,
        out_shape=shapes,
        scratch_shapes=[*(v(a.shape, F32) for a in shapes), pltpu.SemaphoreType.DMA((2, 15))],
        compiler_params=pltpu.CompilerParams(vmem_limit_bytes=60 * 1024 * 1024),
        cost_estimate=pl.CostEstimate(
            flops=0, bytes_accessed=16 * FEAT * COLS, transcendentals=0
        ),
        name="finish",
    )(new_weight, scaled_step, queries, row_factor, col_factor)
    return (
        new_weight, row_factor, col_factor.reshape(COLS), queries, scaled_step,
    )


def solution(mesh):
    placed = (
        P(("mrow", "dp"), "mcol"),
        P("dp", "mrow"),
        P("dp", "mcol"),
        P(),
        P(),
        P("dp", "mrow"),
    )
    return jax.shard_map(
        body,
        mesh=mesh,
        in_specs=placed,
        out_specs=(
            P(("mrow", "dp"), "mcol"),
            P(("mrow", "dp")),
            P("mcol"),
            P(("dp", "mrow"), "mcol"),
            P(("mrow", "dp"), "mcol"),
        ),
        check_vma=False,
    )
```

```python
import jax
import jax.numpy as jnp
from jax import lax
from jax.experimental import pallas as pl
from jax.experimental.pallas import tpu as pltpu
from jax.sharding import PartitionSpec as P

SECOND_DECAY = 1.0 - 10.0 ** (-0.8)
SQUARE_EPS = 1e-30
STEP_RATE = 0.01

NZ = 8
NX = 4
PLANE = 32
TOK = 192
D = 18432
QW = 12288
TOKENS = 1536
FEAT = 288
BLOCK = 2304
COLS = 3072
HALF = 96
QTOK = 24
B_COLS = 128
E_BASE = 512
E_COLS = 768
H_BASE = 2048
H_COLS = 256
WIDTHS = (256,) * 12
STARTS = tuple(sum(WIDTHS[:i]) for i in range(len(WIDTHS)))
NCHUNK = len(WIDTHS)
WMAX = max(WIDTHS)
SLOTS = 4
ORDER = (0, -1, 1, -2, 2, -3, 3, 4)
SLOT = {k % NZ: i for i, k in enumerate(ORDER)}
EARLY = 5 * TOK
LATE = TOKENS - EARLY
N_SEM = 384
MESH = pl.DeviceIdType.MESH
HI = lax.Precision.HIGHEST
F32 = jnp.float32
BF16 = jnp.bfloat16


def rot(base, step, size):
    return lax.rem(base + (step + size) % size, size)


def aligned(start, size, mult):
    return pl.ds(pl.multiple_of(start, mult), size)


def kernel(
    cot_hbm, act_hbm, nxt_hbm, w_hbm, row_old, col_old,
    w_out, s_out, q_out, rf_out, cf_out,
    rs_buf, cs_buf, cot, grad, w_buf, act, act_s, act_all, act_t, act_u, nxt, nxt_s, nxt_y, nxt_all,
    row_acc, row_send, row_recv, vec, vec_z, vec_xy, col_all, scal,
    w_mate, g_mate, row_own, row_mate, w_own, w_peer, part, opp_send, opp_recv, x_send, x_recv, z_send, z_recv,
    local_sem, send_sem, recv_sem,
):
    dp = lax.axis_index("dp")
    mr = lax.axis_index("mrow")
    mc = lax.axis_index("mcol")
    x = lax.rem(mr, NX)
    y = lax.div(mr, NX)
    core = lax.rem(mc, 2)
    sib = {"mcol": mc + 1 - 2 * core}
    ymate = {"mrow": (1 - y) * NX + x}
    count = [0]
    sent = []

    def remote(src, dst, dev, late=True):
        i = count[0]
        count[0] += 1
        copy = pltpu.make_async_remote_copy(
            src_ref=src, dst_ref=dst, send_sem=send_sem.at[i], recv_sem=recv_sem.at[i],
            device_id=dev, device_id_type=MESH,
        )
        copy.start()
        if late:
            sent.append(copy)
        return copy

    def zdev(k):
        return {"dp": rot(dp, k, NZ)}

    def pdev(k):
        place = rot(mr * 4 + mc, k, PLANE)
        return {"mrow": lax.div(place, 4), "mcol": lax.rem(place, 4)}

    def xdev(k):
        return {"mrow": y * NX + rot(x, k, NX)}

    def zrows(k, half=None):
        first = SLOT[k % NZ] * TOK
        if half is None:
            return pl.ds(first, TOK)
        if isinstance(half, int):
            return pl.ds(first + half * HALF, HALF)
        return aligned(first + half * HALF, HALF, 32)

    loads = [
        pltpu.make_async_copy(act_hbm, act, local_sem.at[0]),
        pltpu.make_async_copy(cot_hbm, cot.at[zrows(0)], local_sem.at[1]),
        pltpu.make_async_copy(nxt_hbm, nxt, local_sem.at[2]),
        pltpu.make_async_copy(w_hbm, w_buf, local_sem.at[3]),
    ]
    for load in loads:
        load.start()

    barrier = pltpu.get_barrier_semaphore()
    for k in range(1, NZ):
        pl.semaphore_signal(barrier, inc=1, device_id=zdev(k), device_id_type=MESH)
    for k in range(1, PLANE):
        pl.semaphore_signal(barrier, inc=1, device_id=pdev(k), device_id_type=MESH)
    loads[0].wait()
    for k in range(NZ):
        act_s[k] = act[:, k * FEAT:(k + 1) * FEAT]
    loads[1].wait()
    loads[2].wait()
    for k in range(NZ):
        nxt_s[k] = nxt[:, k * FEAT:(k + 1) * FEAT]
    loads[3].wait()
    pl.semaphore_wait(barrier, NZ + PLANE - 2)

    even = lax.rem(x, 2)
    flows = {
        "h": (H_BASE + (2 * y + even) * H_COLS, H_COLS),
        "b": (x * B_COLS, B_COLS),
        "e": (E_BASE + even * E_COLS, E_COLS // 2),
        "f": (E_BASE + even * E_COLS + E_COLS // 2, E_COLS // 2),
    }
    moves = {"h": (1 - 2 * even) * H_COLS, "e": (1 - 2 * even) * E_COLS}
    moves["f"] = moves["e"]
    z_in = {}

    def z_step(f, s):
        start, width = flows[f]
        cols = aligned(start, width, 128)
        for sign in (1, -1):
            half = None if s < 4 else (1 - sign) // 2
            src = cot.at[zrows(-sign * (s - 1), half), cols]
            dst = cot.at[zrows(-sign * s, half), cols]
            z_in[f, sign, s] = remote(src, dst, zdev(sign))

    def z_next(f, s):
        for sign in (1, -1):
            z_in[f, sign, s].wait_recv()
        if s < 4:
            z_step(f, s + 1)

    def pieces(s):
        return (4,) if s == 4 else (-s, s)

    x_in = {}
    b_in = {}
    y_in = {}

    def x_ref(k, f, half):
        start, width = flows[f]
        return cot.at[zrows(k, half), aligned(start, width, 128)]

    def x_send_pair(f, k):
        for sign in (1, -1):
            ref = x_ref(k, f, (1 - sign) // 2)
            x_in[f, k, sign] = remote(ref, ref, xdev(sign))

    def b_direct(k):
        for sign in (1, -1):
            ref = x_ref(k, "b", None)
            x_in["b", k, sign] = remote(ref, ref, xdev(sign))

    def b_forward(k):
        for sign in (1, -1):
            x_in["b", k, sign].wait_recv()
            ref = cot.at[
                zrows(k, (1 - sign) // 2), aligned(rot(x, -sign, NX) * B_COLS, B_COLS, 128)
            ]
            b_in[k, sign] = remote(ref, ref, xdev(sign))

    def y_own(k):
        ref = x_ref(k, "h", None)
        y_in[k, 0] = remote(ref, ref, ymate)

    def y_other(k):
        for sign in (1, -1):
            x_in["h", k, sign].wait_recv()
        ref = cot.at[zrows(k), aligned(flows["h"][0] + moves["h"], H_COLS, 128)]
        y_in[k, 1] = remote(ref, ref, ymate)

    quarter = core * HALF + lax.div(mc, 2) * (HALF // 2)
    act_in = {}
    act_mid = {}
    act_fwd = {}

    def act_rows(k):
        return aligned(SLOT[k % NZ] * TOK + quarter, HALF // 2, 16)

    def act_send(k):
        act_in[k] = remote(
            act_s.at[rot(dp, k, NZ), aligned(quarter, HALF // 2, 16)],
            act_all.at[act_rows(-k)], zdev(k),
        )

    def act_middle(k):
        act_in[k].wait_recv()
        ref = act_all.at[act_rows(-k)]
        act_mid[k] = remote(ref, ref, {"mcol": rot(mc, 2, 4)})

    def act_forward(k):
        act_mid[k].wait_recv()
        ref = act_all.at[zrows(-k, core)]
        act_fwd[k] = remote(ref, ref, sib)

    for f in ("b", "h", "e", "f"):
        z_step(f, 1)
    early = pl.ds(STARTS[0], WIDTHS[0])
    q_rows = HALF // 2
    nxt_mate = remote(
        nxt_s.at[:, aligned((1 - y) * HALF + core * q_rows, q_rows, 16)], nxt_y, ymate
    )
    for s in range(1, 5):
        if s == 1:
            z_next("b", s)
            for k in pieces(s):
                b_direct(k)
        z_next("h", s)
        for k in pieces(s):
            x_send_pair("h", k)
            y_own(k)
        if s > 1:
            z_next("b", s)
            for k in pieces(s):
                b_direct(k)
        if s == 1:
            for k in (4, 3, 5):
                act_send(k)
            act_all[zrows(0), :] = act_s[dp]

            def weight_square(i, total):
                tile = w_buf[:, aligned(i * 256, 256, 256)]
                return total + jnp.sum((tile * tile).reshape(FEAT // 8, 8, 256), axis=0)

            wsq = lax.fori_loop(0, COLS // 256, weight_square, jnp.zeros((8, 256), F32))
            vec[...] = jnp.zeros((NZ, 8, 128), F32) + jnp.sum(wsq)
            row_acc[...] = jnp.zeros((FEAT, 128), F32)
        if s == 2:
            for k in (2, 6, 1, 7):
                act_send(k)
        if s > 1:
            for k in pieces(s - 1):
                y_other(k)
                b_forward(k)
        if s == 2:
            for k in (4, 3, 5):
                act_middle(k)
        if s == 3:
            for k in (2, 6, 1, 7):
                act_middle(k)
        if s == 4:
            for k in (4, 3, 5, 2, 6, 1, 7):
                act_forward(k)
        for f in ("e", "f"):
            z_next(f, s)
            for k in pieces(s):
                x_send_pair(f, k)

    def nxt_part(z, j):
        return nxt_all.at[j, z, aligned(core * q_rows, q_rows, 16)]

    mine = aligned(y * HALF + core * q_rows, q_rows, 16)
    nxt_in = {}

    def nxt_send(j):
        for k in range(1, NZ):
            src = nxt_s.at[rot(dp, k, NZ), mine] if j == 0 else nxt_y.at[rot(dp, k, NZ)]
            nxt_in[j, k] = remote(src, nxt_part(dp, j), zdev(k))
        nxt_part(dp, j)[...] = nxt_s[dp, mine, :] if j == 0 else nxt_y[dp]

    y_other(4)
    b_forward(4)
    nxt_send(0)
    nxt_mate.wait_recv()
    nxt_send(1)
    mate_w = remote(w_buf.at[:, early], w_mate, ymate, late=False)
    for k in range(1, NZ):
        act_fwd[k].wait_recv()
    for i in (0, 384, 768):
        rows = slice(i, min(i + 384, EARLY))
        act_t[:, rows] = act_all[rows, :].T
    for i in (0, 384):
        rows = slice(i, min(i + 384, LATE))
        act_u[:, rows] = act_all[EARLY + rows.start:EARLY + rows.stop, :].T

    def grad_tiles(base, tiles):
        def one(i, carry):
            start = base + i * 256
            cols = aligned(start, 256, 256)
            g = grad[:, cols] + jnp.dot(
                act_u[...], cot[EARLY:TOKENS, cols], preferred_element_type=F32
            )
            grad[:, cols] = g
            sq = g * g
            row_acc[...] += sq[:, :128] + sq[:, 128:]
            sums = jnp.sum(sq, axis=0, keepdims=True)
            for j in range(2):
                block = lax.div(start, 128) + j
                vec[lax.div(block, 3), pl.ds(lax.rem(block, 3), 1), :] = (
                    sums[:, j * 128:(j + 1) * 128]
                )
            return carry

        lax.fori_loop(0, tiles, one, 0)

    def grad_early(i, carry):
        cols = aligned(i * 256, 256, 256)
        grad[:, cols] = jnp.dot(act_t[...], cot[0:EARLY, cols], preferred_element_type=F32)
        return carry

    for k in ORDER[1:5]:
        for sign in (1, -1):
            b_in[k, sign].wait_recv()
            x_in["e", k, sign].wait_recv()
            x_in["f", k, sign].wait_recv()
        for j in range(2):
            y_in[k, j].wait_recv()
    lax.fori_loop(0, COLS // 256, grad_early, 0)
    every = ORDER[5:]
    grad_tiles(H_BASE + y * 2 * H_COLS, 2 * H_COLS // 256)
    for k in every:
        for sign in (1, -1):
            b_in[k, sign].wait_recv()
    grad_tiles(0, NX * B_COLS // 256)
    grad_tiles(flows["e"][0], E_COLS // 256)
    for k in every:
        for j in range(2):
            y_in[k, j].wait_recv()
    grad_tiles(H_BASE + (1 - y) * 2 * H_COLS, 2 * H_COLS // 256)
    for k in every:
        for sign in (1, -1):
            x_in["e", k, sign].wait_recv()
            x_in["f", k, sign].wait_recv()
    grad_tiles(flows["e"][0] + moves["e"], E_COLS // 256)

    ones = jnp.ones((8, 128), F32)
    row_send[...] = lax.dot_general(
        ones, row_acc[...], (((1,), (1,)), ((), ())), precision=HI, preferred_element_type=F32
    )
    row_in = [
        remote(row_send, row_recv.at[k], {"mcol": rot(mc, k, 4)}) for k in range(1, 4)
    ]
    mate_g = remote(grad.at[:, early], g_mate, ymate, late=False)
    place = (mr * NZ + dp) * (FEAT // 32)
    first = lax.div(place, 4)
    shift = lax.rem(place, 4)
    near = jnp.concatenate([row_old[pl.ds(first + j, 1), :] for j in range(3)], axis=1)
    row_mine = near[:, 0:FEAT]
    for j in range(1, 4):
        row_mine = jnp.where(shift == j, near[:, j * 32:j * 32 + FEAT], row_mine)
    for copy in row_in:
        copy.wait_recv()
    row_full = ((row_send[...] + row_recv[1]) + row_recv[2]) + row_recv[3]
    row_factor = SECOND_DECAY * row_mine + (1.0 - SECOND_DECAY) * (
        row_full * (1.0 / QW) + SQUARE_EPS
    )
    rf_out[...] = row_factor[0]
    row_own[...] = row_factor
    mate_r = remote(row_own, row_mate, ymate)
    row_inv = lax.dot_general(
        1.0 / row_factor, ones * 0.125, (((0,), (0,)), ((), ())), precision=HI,
        preferred_element_type=F32,
    )

    def weighted(i, carry):
        for j in range(2):
            block = i * 2 + j
            g = grad[:, aligned(block * 128, 128, 128)]
            vec[lax.div(block, 3), pl.ds(3 + lax.rem(block, 3), 1), :] = (
                jnp.sum(g * g * row_inv, axis=0, keepdims=True)
            )
        return carry

    lax.fori_loop(0, COLS // 256, weighted, 0)

    sum_in = [
        remote(vec.at[rot(dp, k, NZ)], vec_z.at[k], zdev(k)) for k in range(1, NZ)
    ]
    total = vec[dp]
    for k in range(1, NZ):
        sum_in[k - 1].wait_recv()
        total = total + vec_z[k]
    vec_xy[0] = total
    sum_in = [
        remote(vec_xy.at[0], vec_xy.at[k], pdev(k)) for k in range(1, PLANE)
    ]
    old = []
    for d in range(4):
        base = rot(mc, -d, 4) * 24 + dp * 3
        old.append(jnp.concatenate(
            [col_old[pl.ds(base + j, 1), :] for j in range(3)], axis=0
        ))
    totals = [total, None, None, None]
    for k in range(1, PLANE):
        sum_in[k - 1].wait_recv()
    for k in range(1, PLANE):
        d = k % 4
        totals[d] = vec_xy[k] if totals[d] is None else totals[d] + vec_xy[k]
    square = jnp.zeros((3, 128), F32)
    moved = jnp.zeros((3, 128), F32)
    col_part = []
    for d in range(4):
        col_part.append(SECOND_DECAY * old[d] + (1.0 - SECOND_DECAY) * (
            totals[d][0:3] * (1.0 / D) + SQUARE_EPS
        ))
        square = square + totals[d][0:3]
        moved = moved + totals[d][3:6] / col_part[d]
    w_total = ((totals[0] + totals[1]) + totals[2]) + totals[3]
    scal[...] = jnp.zeros((8, 128), F32)
    scal[0:3] = col_part[0]
    scal[3:4] = jnp.sum(square, axis=0, keepdims=True)
    scal[4:5] = jnp.sum(moved, axis=0, keepdims=True)
    sum_in = [
        remote(scal, col_all.at[dp], zdev(k)) for k in range(1, NZ)
    ]
    col_all[dp] = scal[...]
    nxt_fwd = []
    for j in range(2):
        for k in range(1, NZ):
            nxt_in[j, k].wait_recv()
        ref = nxt_all.at[j, :, aligned(core * q_rows, q_rows, 16)]
        nxt_fwd.append(remote(ref, ref, sib))
    old_total = jnp.sum(row_old[...])
    row_root = jnp.sqrt(row_inv)
    for copy in sum_in:
        copy.wait_recv()
    sums = col_all[0]
    for k in range(1, NZ):
        sums = sums + col_all[k]
    for k in range(NZ):
        for j in range(3):
            cols = slice((k * 3 + j) * 128, (k * 3 + j + 1) * 128)
            cf_out[:, cols] = col_all[k, j:j + 1, :]
    cs_buf[...] = lax.rsqrt(cf_out[...])
    square_total = jnp.sum(sums[3:4], axis=1, keepdims=True)
    moved_total = jnp.sum(sums[4:5], axis=1, keepdims=True)
    row_mean = (
        SECOND_DECAY * old_total
        + (1.0 - SECOND_DECAY) * (square_total * (1.0 / QW) + D * SQUARE_EPS)
    ) * (1.0 / D)
    entries = float(D) * float(QW)
    clip = jnp.maximum(1.0, jnp.sqrt(row_mean * moved_total * (1.0 / entries)))
    w_scale = jnp.sqrt(w_total[6:7, 0:1] * (1.0 / entries))
    scale = w_scale * jnp.sqrt(row_mean) / clip
    rs_buf[...] = row_root * scale

    mate_w.wait()
    mate_g.wait()
    mate_r.wait_recv()
    mate_scale = scale * jnp.sqrt(lax.dot_general(
        1.0 / row_mate[...], ones * 0.125, (((0,), (0,)), ((), ())), precision=HI,
        preferred_element_type=F32,
    ))
    for i in range(WIDTHS[0] // 128):
        cols = slice(i * 128, (i + 1) * 128)
        step = g_mate[:, cols] * (mate_scale * cs_buf[0:1, cols])
        w_peer[:, cols] = (w_mate[:, cols] - STEP_RATE * step).astype(BF16)
    w_in = []
    for c in (*range(1, NCHUNK), 0):
        def update(i, carry, c=c):
            cols = aligned(STARTS[c] + i * 128, 128, 128)
            step = grad[:, cols] * (rs_buf[...] * cs_buf[0:1, cols])
            new_w = w_buf[:, cols] - STEP_RATE * step
            grad[:, cols] = step
            w_buf[:, cols] = new_w
            w_own[:, cols] = new_w.astype(BF16)
            return carry

        lax.fori_loop(0, WIDTHS[c] // 128, update, 0)
        if c > 0:
            cols = pl.ds(STARTS[c], WIDTHS[c])
            w_in.append(remote(w_own.at[:, cols], w_peer.at[:, cols], ymate))
    outs = [
        pltpu.make_async_copy(w_buf, w_out, local_sem.at[4]),
        pltpu.make_async_copy(grad, s_out, local_sem.at[5]),
    ]
    for copy in outs:
        copy.start()
    for copy in nxt_fwd:
        copy.wait_recv()

    opp_in = {}
    q_in = {}
    z_part = {}
    x_next = rot(x, 1, NX)
    x_prev = rot(x, 3, NX)
    x_opp = rot(x, 2, NX)

    def block(c, q, lo, hi):
        return part[c % SLOTS, :, q, :, lo:hi].reshape(NZ * QTOK, hi - lo)

    def stage_matmul(c):
        if c > 0:
            w_in[c - 1].wait_recv()
        width = WIDTHS[c]
        hw = width // 2

        def one(i, carry):
            src = aligned(STARTS[c] + i * 256, 256, 256)
            for r in range(2):
                zs = slice(r * 4, (r + 1) * 4)
                p = jnp.dot(
                    nxt_all[0, zs].reshape(4 * HALF, FEAT), w_own[:, src],
                    preferred_element_type=F32,
                )
                p = p + jnp.dot(
                    nxt_all[1, zs].reshape(4 * HALF, FEAT), w_peer[:, src],
                    preferred_element_type=F32,
                )
                part[c % SLOTS, zs, :, :, aligned(i * 256, 256, 256)] = (
                    p.reshape(4, NX, QTOK, 256)
                )
            return carry

        lax.fori_loop(0, width // 256, one, 0)
        cols = pl.ds(STARTS[c] // 2, hw)
        for j, sign in ((0, 1), (1, -1)):
            opp_send[j, :, cols] = block(c, x_opp, j * hw, (j + 1) * hw).astype(BF16)
            opp_in[c, j] = remote(
                opp_send.at[j, :, cols], opp_recv.at[j, :, cols],
                xdev(sign),
            )

    def stage_relay(c):
        width = WIDTHS[c]
        hw = width // 2
        base = STARTS[c]
        cols = pl.ds(base // 2, hw)
        for j, sign, q in ((0, 1, x_next), (1, -1, x_prev)):
            opp_in[c, j].wait_recv()
            lo = j * hw
            x_send[j, :, base + lo:base + lo + hw] = (
                block(c, q, lo, lo + hw) + opp_recv[j, :, cols].astype(F32)
            ).astype(BF16)
            lo = hw - lo
            x_send[j, :, base + lo:base + lo + hw] = block(c, q, lo, lo + hw).astype(BF16)
            full = pl.ds(base, width)
            q_in[c, j] = remote(x_send.at[j, :, full], x_recv.at[j, :, full], xdev(sign))

    def stage_z(c):
        width = WIDTHS[c]
        hw = width // 2
        base = STARTS[c]
        q_in[c, 0].wait_recv()
        q_in[c, 1].wait_recv()
        full = slice(base, base + width)
        summed = (
            block(c, x, 0, width)
            + x_recv[0, :, full].astype(F32) + x_recv[1, :, full].astype(F32)
        ).reshape(NZ, QTOK, width)
        part[c % SLOTS, :, x, :, 0:width] = summed
        cols = pl.ds(base // 2, hw)
        z_send[:, :, cols] = jnp.concatenate(
            [summed[:, :, :hw], summed[:, :, hw:]], axis=1
        ).astype(BF16)
        for k in range(1, NZ):
            z_part[c, k] = remote(
                z_send.at[rot(dp, k, NZ), :, cols], z_recv.at[k, :, cols], zdev(k)
            )
        q_out[:, full] = part[c % SLOTS, dp, x, :, 0:width]

    def stage_out(c):
        hw = WIDTHS[c] // 2
        acc = None
        for k in range(1, NZ):
            z_part[c, k].wait_recv()
            term = z_recv[k, :, pl.ds(STARTS[c] // 2, hw)].astype(F32)
            acc = term if acc is None else acc + term
        for j in range(2):
            cols = pl.ds(STARTS[c] + j * hw, hw)
            q_out[:, cols] = (q_out[:, cols] + acc[j * QTOK:(j + 1) * QTOK]) * D ** (-0.5)

    for t in range(NCHUNK):
        stage_matmul(t)
        if t >= 1:
            stage_relay(t - 1)
        if t >= 3:
            stage_z(t - 3)
        if t >= 5:
            stage_out(t - 5)
    stage_relay(NCHUNK - 1)
    for t in range(NCHUNK - 3, NCHUNK):
        stage_z(t)
    for t in range(NCHUNK - 5, NCHUNK):
        stage_out(t)

    for copy in outs:
        copy.wait()
    for copy in sent:
        copy.wait_send()
    assert count[0] <= N_SEM


def finish(*refs):
    src, dst, buf, sem = refs[:5], refs[5:10], refs[10:15], refs[15]
    views = []
    for i in range(2):
        for r in range(6):
            views.append((i, pl.ds(r * 48, 48)))
    views += [(i, slice(None)) for i in range(2, 5)]
    into = [
        pltpu.make_async_copy(src[i].at[rows], buf[i].at[rows], sem.at[0, n])
        for n, (i, rows) in enumerate(views)
    ]
    out = [
        pltpu.make_async_copy(buf[i].at[rows], dst[i].at[rows], sem.at[1, n])
        for n, (i, rows) in enumerate(views)
    ]
    for copy in into:
        copy.start()
    for first, second in zip(into, out):
        first.wait()
        second.start()
    for copy in out:
        copy.wait()


def body(weight, activations, cotangent, row_old, col_old, next_input):
    vm = pl.BlockSpec(memory_space=pltpu.VMEM)
    hbm = pl.BlockSpec(memory_space=pl.ANY)
    v = pltpu.VMEM

    def shape(*dims):
        return jax.ShapeDtypeStruct(dims, F32)

    new_weight, scaled_step, queries, row_factor, col_factor = pl.pallas_call(
        kernel,
        out_shape=(
            shape(FEAT, COLS), shape(FEAT, COLS), shape(QTOK, COLS), shape(FEAT),
            shape(1, COLS),
        ),
        in_specs=[hbm, hbm, hbm, hbm, vm, vm],
        out_specs=(hbm, hbm, vm, vm, vm),
        scratch_shapes=[
            v((FEAT, 128), F32),
            v((1, COLS), F32),
            v((TOKENS, COLS), BF16),
            v((FEAT, COLS), F32),
            v((FEAT, COLS), F32),
            v((TOK, BLOCK), BF16),
            v((NZ, TOK, FEAT), BF16),
            v((TOKENS, FEAT), BF16),
            v((FEAT, EARLY), BF16),
            v((FEAT, LATE), BF16),
            v((TOK, BLOCK), BF16),
            v((NZ, TOK, FEAT), BF16),
            v((NZ, HALF // 2, FEAT), BF16),
            v((2, NZ, HALF, FEAT), BF16),
            v((FEAT, 128), F32),
            v((8, FEAT), F32),
            v((4, 8, FEAT), F32),
            v((NZ, 8, 128), F32),
            v((NZ, 8, 128), F32),
            v((PLANE, 8, 128), F32),
            v((NZ, 8, 128), F32),
            v((8, 128), F32),
            v((FEAT, WIDTHS[0]), F32),
            v((FEAT, WIDTHS[0]), F32),
            v((8, FEAT), F32),
            v((8, FEAT), F32),
            v((FEAT, COLS), BF16),
            v((FEAT, COLS), BF16),
            v((SLOTS, NZ, NX, QTOK, WMAX), F32),
            v((2, TOK, COLS // 2), BF16),
            v((2, TOK, COLS // 2), BF16),
            v((2, TOK, COLS), BF16),
            v((2, TOK, COLS), BF16),
            v((NZ, 2 * QTOK, COLS // 2), BF16),
            v((NZ, 2 * QTOK, COLS // 2), BF16),
            pltpu.SemaphoreType.DMA((6,)),
            pltpu.SemaphoreType.DMA((N_SEM,)),
            pltpu.SemaphoreType.DMA((N_SEM,)),
        ],
        compiler_params=pltpu.CompilerParams(
            collective_id=0, has_side_effects=True, vmem_limit_bytes=60 * 1024 * 1024
        ),
        cost_estimate=pl.CostEstimate(
            flops=4 * TOKENS * FEAT * COLS, bytes_accessed=16_000_000, transcendentals=0
        ),
        name="update",
    )(
        cotangent, activations, next_input, weight,
        row_old.reshape(D // 128, 128), col_old.reshape(QW // 128, 128),
    )
    shapes = (
        shape(FEAT, COLS), shape(FEAT, COLS), shape(QTOK, COLS), shape(FEAT),
        shape(1, COLS),
    )
    new_weight, scaled_step, queries, row_factor, col_factor = pl.pallas_call(
        finish,
        in_specs=[hbm] * 5,
        out_specs=(hbm,) * 5,
        out_shape=shapes,
        scratch_shapes=[*(v(a.shape, F32) for a in shapes), pltpu.SemaphoreType.DMA((2, 15))],
        compiler_params=pltpu.CompilerParams(vmem_limit_bytes=60 * 1024 * 1024),
        cost_estimate=pl.CostEstimate(
            flops=0, bytes_accessed=16 * FEAT * COLS, transcendentals=0
        ),
        name="finish",
    )(new_weight, scaled_step, queries, row_factor, col_factor)
    return (
        new_weight, row_factor, col_factor.reshape(COLS), queries, scaled_step,
    )


def solution(mesh):
    placed = (
        P(("mrow", "dp"), "mcol"),
        P("dp", "mrow"),
        P("dp", "mcol"),
        P(),
        P(),
        P("dp", "mrow"),
    )
    return jax.shard_map(
        body,
        mesh=mesh,
        in_specs=placed,
        out_specs=(
            P(("mrow", "dp"), "mcol"),
            P(("mrow", "dp")),
            P("mcol"),
            P(("dp", "mrow"), "mcol"),
            P(("mrow", "dp"), "mcol"),
        ),
        check_vma=False,
    )
```

```python
import jax
import jax.numpy as jnp
from jax import lax
from jax.experimental import pallas as pl
from jax.experimental.pallas import tpu as pltpu
from jax.sharding import PartitionSpec as P

SECOND_DECAY = 1.0 - 10.0 ** (-0.8)
SQUARE_EPS = 1e-30
STEP_RATE = 0.01

NZ = 8
NX = 4
PLANE = 32
TOK = 192
D = 18432
QW = 12288
TOKENS = 1536
FEAT = 288
BLOCK = 2304
COLS = 3072
HALF = 96
QTOK = 24
B_COLS = 128
E_BASE = 512
E_COLS = 768
H_BASE = 2048
H_COLS = 256
WIDTHS = (256,) * 12
STARTS = tuple(sum(WIDTHS[:i]) for i in range(len(WIDTHS)))
NCHUNK = len(WIDTHS)
WMAX = max(WIDTHS)
SLOTS = 4
ORDER = (0, -1, 1, -2, 2, -3, 3, 4)
SLOT = {k % NZ: i for i, k in enumerate(ORDER)}
EARLY = 5 * TOK
LATE = TOKENS - EARLY
N_SEM = 384
MESH = pl.DeviceIdType.MESH
HI = lax.Precision.HIGHEST
F32 = jnp.float32
BF16 = jnp.bfloat16


def rot(base, step, size):
    return lax.rem(base + (step + size) % size, size)


def aligned(start, size, mult):
    return pl.ds(pl.multiple_of(start, mult), size)


def kernel(
    cot_hbm, act_hbm, nxt_hbm, w_hbm, row_old, col_old,
    w_out, s_out, q_out, rf_out, cf_out,
    rs_buf, cs_buf, cot, grad, w_buf, act, act_s, act_all, act_t, act_u, nxt, nxt_s, nxt_y, nxt_all,
    row_acc, row_send, row_recv, vec, vec_z, vec_xy, col_all, scal,
    w_mate, g_mate, row_own, row_mate, w_own, w_peer, part, opp_send, opp_recv, x_send, x_recv, z_send, z_recv,
    local_sem, send_sem, recv_sem,
):
    dp = lax.axis_index("dp")
    mr = lax.axis_index("mrow")
    mc = lax.axis_index("mcol")
    x = lax.rem(mr, NX)
    y = lax.div(mr, NX)
    core = lax.rem(mc, 2)
    sib = {"mcol": mc + 1 - 2 * core}
    ymate = {"mrow": (1 - y) * NX + x}
    count = [0]
    sent = []

    def remote(src, dst, dev, late=True):
        i = count[0]
        count[0] += 1
        copy = pltpu.make_async_remote_copy(
            src_ref=src, dst_ref=dst, send_sem=send_sem.at[i], recv_sem=recv_sem.at[i],
            device_id=dev, device_id_type=MESH,
        )
        copy.start()
        if late:
            sent.append(copy)
        return copy

    def zdev(k):
        return {"dp": rot(dp, k, NZ)}

    def pdev(k):
        place = rot(mr * 4 + mc, k, PLANE)
        return {"mrow": lax.div(place, 4), "mcol": lax.rem(place, 4)}

    def xdev(k):
        return {"mrow": y * NX + rot(x, k, NX)}

    def zrows(k, half=None):
        first = SLOT[k % NZ] * TOK
        if half is None:
            return pl.ds(first, TOK)
        if isinstance(half, int):
            return pl.ds(first + half * HALF, HALF)
        return aligned(first + half * HALF, HALF, 32)

    loads = [
        pltpu.make_async_copy(act_hbm, act, local_sem.at[0]),
        pltpu.make_async_copy(cot_hbm, cot.at[zrows(0)], local_sem.at[1]),
        pltpu.make_async_copy(nxt_hbm, nxt, local_sem.at[2]),
        pltpu.make_async_copy(w_hbm, w_buf, local_sem.at[3]),
    ]
    for load in loads:
        load.start()

    barrier = pltpu.get_barrier_semaphore()
    for k in range(1, NZ):
        pl.semaphore_signal(barrier, inc=1, device_id=zdev(k), device_id_type=MESH)
    for k in range(1, PLANE):
        pl.semaphore_signal(barrier, inc=1, device_id=pdev(k), device_id_type=MESH)
    loads[0].wait()
    for k in range(NZ):
        act_s[k] = act[:, k * FEAT:(k + 1) * FEAT]
    loads[1].wait()
    loads[2].wait()
    for k in range(NZ):
        nxt_s[k] = nxt[:, k * FEAT:(k + 1) * FEAT]
    loads[3].wait()
    pl.semaphore_wait(barrier, NZ + PLANE - 2)

    even = lax.rem(x, 2)
    flows = {
        "h": (H_BASE + (2 * y + even) * H_COLS, H_COLS),
        "b": (x * B_COLS, B_COLS),
        "e": (E_BASE + even * E_COLS, E_COLS // 2),
        "f": (E_BASE + even * E_COLS + E_COLS // 2, E_COLS // 2),
    }
    moves = {"h": (1 - 2 * even) * H_COLS, "e": (1 - 2 * even) * E_COLS}
    moves["f"] = moves["e"]
    z_in = {}

    def z_step(f, s):
        start, width = flows[f]
        cols = aligned(start, width, 128)
        for sign in (1, -1):
            half = None if s < 4 else (1 - sign) // 2
            src = cot.at[zrows(-sign * (s - 1), half), cols]
            dst = cot.at[zrows(-sign * s, half), cols]
            z_in[f, sign, s] = remote(src, dst, zdev(sign))

    def z_next(f, s):
        for sign in (1, -1):
            z_in[f, sign, s].wait_recv()
        if s < 4:
            z_step(f, s + 1)

    def pieces(s):
        return (4,) if s == 4 else (-s, s)

    x_in = {}
    b_in = {}
    y_in = {}

    def x_ref(k, f, half):
        start, width = flows[f]
        return cot.at[zrows(k, half), aligned(start, width, 128)]

    def x_send_pair(f, k):
        for sign in (1, -1):
            ref = x_ref(k, f, (1 - sign) // 2)
            x_in[f, k, sign] = remote(ref, ref, xdev(sign))

    def b_direct(k):
        for sign in (1, -1):
            ref = x_ref(k, "b", None)
            x_in["b", k, sign] = remote(ref, ref, xdev(sign))

    def b_forward(k):
        for sign in (1, -1):
            x_in["b", k, sign].wait_recv()
            ref = cot.at[
                zrows(k, (1 - sign) // 2), aligned(rot(x, -sign, NX) * B_COLS, B_COLS, 128)
            ]
            b_in[k, sign] = remote(ref, ref, xdev(sign))

    def y_own(k):
        ref = x_ref(k, "h", None)
        y_in[k, 0] = remote(ref, ref, ymate)

    def y_other(k):
        for sign in (1, -1):
            x_in["h", k, sign].wait_recv()
        ref = cot.at[zrows(k), aligned(flows["h"][0] + moves["h"], H_COLS, 128)]
        y_in[k, 1] = remote(ref, ref, ymate)

    quarter = core * HALF + lax.div(mc, 2) * (HALF // 2)
    act_in = {}
    act_mid = {}
    act_fwd = {}

    def act_rows(k):
        return aligned(SLOT[k % NZ] * TOK + quarter, HALF // 2, 16)

    def act_send(k):
        act_in[k] = remote(
            act_s.at[rot(dp, k, NZ), aligned(quarter, HALF // 2, 16)],
            act_all.at[act_rows(-k)], zdev(k),
        )

    def act_middle(k):
        act_in[k].wait_recv()
        ref = act_all.at[act_rows(-k)]
        act_mid[k] = remote(ref, ref, {"mcol": rot(mc, 2, 4)})

    def act_forward(k):
        act_mid[k].wait_recv()
        ref = act_all.at[zrows(-k, core)]
        act_fwd[k] = remote(ref, ref, sib)

    for f in ("b", "h", "e", "f"):
        z_step(f, 1)
    early = pl.ds(STARTS[0], WIDTHS[0])
    q_rows = HALF // 2
    nxt_mate = remote(
        nxt_s.at[:, aligned((1 - y) * HALF + core * q_rows, q_rows, 16)], nxt_y, ymate
    )
    for s in range(1, 5):
        if s == 1:
            z_next("b", s)
            for k in pieces(s):
                b_direct(k)
        z_next("h", s)
        for k in pieces(s):
            x_send_pair("h", k)
            y_own(k)
        if s > 1:
            z_next("b", s)
            for k in pieces(s):
                b_direct(k)
        if s == 1:
            for k in (4, 3, 5):
                act_send(k)
            act_all[zrows(0), :] = act_s[dp]

            def weight_square(i, total):
                tile = w_buf[:, aligned(i * 256, 256, 256)]
                return total + jnp.sum((tile * tile).reshape(FEAT // 8, 8, 256), axis=0)

            wsq = lax.fori_loop(0, COLS // 256, weight_square, jnp.zeros((8, 256), F32))
            vec[...] = jnp.zeros((NZ, 8, 128), F32) + jnp.sum(wsq)
            row_acc[...] = jnp.zeros((FEAT, 128), F32)
        if s == 2:
            for k in (2, 6, 1, 7):
                act_send(k)
        if s > 1:
            for k in pieces(s - 1):
                y_other(k)
                b_forward(k)
        if s == 2:
            for k in (4, 3, 5):
                act_middle(k)
        if s == 3:
            for k in (2, 6, 1, 7):
                act_middle(k)
        if s == 4:
            for k in (4, 3, 5, 2, 6, 1, 7):
                act_forward(k)
        for f in ("e", "f"):
            z_next(f, s)
            for k in pieces(s):
                x_send_pair(f, k)

    def nxt_part(z, j):
        return nxt_all.at[j, z, aligned(core * q_rows, q_rows, 16)]

    mine = aligned(y * HALF + core * q_rows, q_rows, 16)
    nxt_in = {}

    def nxt_send(j):
        for k in range(1, NZ):
            src = nxt_s.at[rot(dp, k, NZ), mine] if j == 0 else nxt_y.at[rot(dp, k, NZ)]
            nxt_in[j, k] = remote(src, nxt_part(dp, j), zdev(k))
        nxt_part(dp, j)[...] = nxt_s[dp, mine, :] if j == 0 else nxt_y[dp]

    y_other(4)
    b_forward(4)
    nxt_send(0)
    nxt_mate.wait_recv()
    nxt_send(1)
    mate_w = remote(w_buf.at[:, early], w_mate, ymate, late=False)
    for k in range(1, NZ):
        act_fwd[k].wait_recv()
    for i in (0, 384, 768):
        rows = slice(i, min(i + 384, EARLY))
        act_t[:, rows] = act_all[rows, :].T
    for i in (0, 384):
        rows = slice(i, min(i + 384, LATE))
        act_u[:, rows] = act_all[EARLY + rows.start:EARLY + rows.stop, :].T

    def grad_tiles(base, tiles):
        def one(i, carry):
            start = base + i * 256
            cols = aligned(start, 256, 256)
            g = grad[:, cols] + jnp.dot(
                act_u[...], cot[EARLY:TOKENS, cols], preferred_element_type=F32
            )
            grad[:, cols] = g
            sq = g * g
            row_acc[...] += sq[:, :128] + sq[:, 128:]
            sums = jnp.sum(sq, axis=0, keepdims=True)
            for j in range(2):
                block = lax.div(start, 128) + j
                vec[lax.div(block, 3), pl.ds(lax.rem(block, 3), 1), :] = (
                    sums[:, j * 128:(j + 1) * 128]
                )
            return carry

        lax.fori_loop(0, tiles, one, 0)

    def grad_early(i, carry):
        cols = aligned(i * 256, 256, 256)
        grad[:, cols] = jnp.dot(act_t[...], cot[0:EARLY, cols], preferred_element_type=F32)
        return carry

    for k in ORDER[1:5]:
        for sign in (1, -1):
            b_in[k, sign].wait_recv()
            x_in["e", k, sign].wait_recv()
            x_in["f", k, sign].wait_recv()
        for j in range(2):
            y_in[k, j].wait_recv()
    lax.fori_loop(0, COLS // 256, grad_early, 0)
    every = ORDER[5:]
    grad_tiles(H_BASE + y * 2 * H_COLS, 2 * H_COLS // 256)
    for k in every:
        for sign in (1, -1):
            b_in[k, sign].wait_recv()
    grad_tiles(0, NX * B_COLS // 256)
    grad_tiles(flows["e"][0], E_COLS // 256)
    for k in every:
        for j in range(2):
            y_in[k, j].wait_recv()
    grad_tiles(H_BASE + (1 - y) * 2 * H_COLS, 2 * H_COLS // 256)
    for k in every:
        for sign in (1, -1):
            x_in["e", k, sign].wait_recv()
            x_in["f", k, sign].wait_recv()
    grad_tiles(flows["e"][0] + moves["e"], E_COLS // 256)

    ones = jnp.ones((8, 128), F32)
    row_send[...] = lax.dot_general(
        ones, row_acc[...], (((1,), (1,)), ((), ())), precision=HI, preferred_element_type=F32
    )
    row_in = [
        remote(row_send, row_recv.at[k], {"mcol": rot(mc, k, 4)}) for k in range(1, 4)
    ]
    mate_g = remote(grad.at[:, early], g_mate, ymate, late=False)
    place = (mr * NZ + dp) * (FEAT // 32)
    first = lax.div(place, 4)
    shift = lax.rem(place, 4)
    near = jnp.concatenate([row_old[pl.ds(first + j, 1), :] for j in range(3)], axis=1)
    row_mine = near[:, 0:FEAT]
    for j in range(1, 4):
        row_mine = jnp.where(shift == j, near[:, j * 32:j * 32 + FEAT], row_mine)
    for copy in row_in:
        copy.wait_recv()
    row_full = ((row_send[...] + row_recv[1]) + row_recv[2]) + row_recv[3]
    row_factor = SECOND_DECAY * row_mine + (1.0 - SECOND_DECAY) * (
        row_full * (1.0 / QW) + SQUARE_EPS
    )
    rf_out[...] = row_factor[0]
    row_own[...] = row_factor
    mate_r = remote(row_own, row_mate, ymate)
    row_inv = lax.dot_general(
        1.0 / row_factor, ones * 0.125, (((0,), (0,)), ((), ())), precision=HI,
        preferred_element_type=F32,
    )

    def weighted(i, carry):
        for j in range(2):
            block = i * 2 + j
            g = grad[:, aligned(block * 128, 128, 128)]
            vec[lax.div(block, 3), pl.ds(3 + lax.rem(block, 3), 1), :] = (
                jnp.sum(g * g * row_inv, axis=0, keepdims=True)
            )
        return carry

    lax.fori_loop(0, COLS // 256, weighted, 0)

    sum_in = [
        remote(vec.at[rot(dp, k, NZ)], vec_z.at[k], zdev(k)) for k in range(1, NZ)
    ]
    total = vec[dp]
    for k in range(1, NZ):
        sum_in[k - 1].wait_recv()
        total = total + vec_z[k]
    vec_xy[0] = total
    sum_in = [
        remote(vec_xy.at[0], vec_xy.at[k], pdev(k)) for k in range(1, PLANE)
    ]
    old = []
    for d in range(4):
        base = rot(mc, -d, 4) * 24 + dp * 3
        old.append(jnp.concatenate(
            [col_old[pl.ds(base + j, 1), :] for j in range(3)], axis=0
        ))
    totals = [total, None, None, None]
    for k in range(1, PLANE):
        sum_in[k - 1].wait_recv()
    for k in range(1, PLANE):
        d = k % 4
        totals[d] = vec_xy[k] if totals[d] is None else totals[d] + vec_xy[k]
    square = jnp.zeros((3, 128), F32)
    moved = jnp.zeros((3, 128), F32)
    col_part = []
    for d in range(4):
        col_part.append(SECOND_DECAY * old[d] + (1.0 - SECOND_DECAY) * (
            totals[d][0:3] * (1.0 / D) + SQUARE_EPS
        ))
        square = square + totals[d][0:3]
        moved = moved + totals[d][3:6] / col_part[d]
    w_total = ((totals[0] + totals[1]) + totals[2]) + totals[3]
    scal[...] = jnp.zeros((8, 128), F32)
    scal[0:3] = col_part[0]
    scal[3:4] = jnp.sum(square, axis=0, keepdims=True)
    scal[4:5] = jnp.sum(moved, axis=0, keepdims=True)
    sum_in = [
        remote(scal, col_all.at[dp], zdev(k)) for k in range(1, NZ)
    ]
    col_all[dp] = scal[...]
    nxt_fwd = []
    for j in range(2):
        for k in range(1, NZ):
            nxt_in[j, k].wait_recv()
        ref = nxt_all.at[j, :, aligned(core * q_rows, q_rows, 16)]
        nxt_fwd.append(remote(ref, ref, sib))
    old_total = jnp.sum(row_old[...])
    row_root = jnp.sqrt(row_inv)
    for copy in sum_in:
        copy.wait_recv()
    sums = col_all[0]
    for k in range(1, NZ):
        sums = sums + col_all[k]
    for k in range(NZ):
        for j in range(3):
            cols = slice((k * 3 + j) * 128, (k * 3 + j + 1) * 128)
            cf_out[:, cols] = col_all[k, j:j + 1, :]
    cs_buf[...] = lax.rsqrt(cf_out[...])
    square_total = jnp.sum(sums[3:4], axis=1, keepdims=True)
    moved_total = jnp.sum(sums[4:5], axis=1, keepdims=True)
    row_mean = (
        SECOND_DECAY * old_total
        + (1.0 - SECOND_DECAY) * (square_total * (1.0 / QW) + D * SQUARE_EPS)
    ) * (1.0 / D)
    entries = float(D) * float(QW)
    clip = jnp.maximum(1.0, jnp.sqrt(row_mean * moved_total * (1.0 / entries)))
    w_scale = jnp.sqrt(w_total[6:7, 0:1] * (1.0 / entries))
    scale = w_scale * jnp.sqrt(row_mean) / clip
    rs_buf[...] = row_root * scale

    mate_w.wait()
    mate_g.wait()
    mate_r.wait_recv()
    mate_scale = scale * jnp.sqrt(lax.dot_general(
        1.0 / row_mate[...], ones * 0.125, (((0,), (0,)), ((), ())), precision=HI,
        preferred_element_type=F32,
    ))
    for i in range(WIDTHS[0] // 128):
        cols = slice(i * 128, (i + 1) * 128)
        step = g_mate[:, cols] * (mate_scale * cs_buf[0:1, cols])
        w_peer[:, cols] = (w_mate[:, cols] - STEP_RATE * step).astype(BF16)
    w_in = []

    def refresh(c):
        def update(i, carry):
            cols = aligned(STARTS[c] + i * 128, 128, 128)
            step = grad[:, cols] * (rs_buf[...] * cs_buf[0:1, cols])
            new_w = w_buf[:, cols] - STEP_RATE * step
            grad[:, cols] = step
            w_buf[:, cols] = new_w
            w_own[:, cols] = new_w.astype(BF16)
            return carry

        lax.fori_loop(0, WIDTHS[c] // 128, update, 0)
        if c > 0:
            cols = pl.ds(STARTS[c], WIDTHS[c])
            w_in.append(remote(w_own.at[:, cols], w_peer.at[:, cols], ymate))

    for c in (1, 2, 3, 0):
        refresh(c)
    for copy in nxt_fwd:
        copy.wait_recv()

    opp_in = {}
    q_in = {}
    z_part = {}
    x_next = rot(x, 1, NX)
    x_prev = rot(x, 3, NX)
    x_opp = rot(x, 2, NX)

    def block(c, q, lo, hi):
        return part[c % SLOTS, :, q, :, lo:hi].reshape(NZ * QTOK, hi - lo)

    def stage_matmul(c):
        if c > 0:
            w_in[c - 1].wait_recv()
        width = WIDTHS[c]
        hw = width // 2

        def one(i, carry):
            src = aligned(STARTS[c] + i * 256, 256, 256)
            for r in range(2):
                zs = slice(r * 4, (r + 1) * 4)
                p = jnp.dot(
                    nxt_all[0, zs].reshape(4 * HALF, FEAT), w_own[:, src],
                    preferred_element_type=F32,
                )
                p = p + jnp.dot(
                    nxt_all[1, zs].reshape(4 * HALF, FEAT), w_peer[:, src],
                    preferred_element_type=F32,
                )
                part[c % SLOTS, zs, :, :, aligned(i * 256, 256, 256)] = (
                    p.reshape(4, NX, QTOK, 256)
                )
            return carry

        lax.fori_loop(0, width // 256, one, 0)
        cols = pl.ds(STARTS[c] // 2, hw)
        for j, sign in ((0, 1), (1, -1)):
            opp_send[j, :, cols] = block(c, x_opp, j * hw, (j + 1) * hw).astype(BF16)
            opp_in[c, j] = remote(
                opp_send.at[j, :, cols], opp_recv.at[j, :, cols],
                xdev(sign),
            )

    def stage_relay(c):
        width = WIDTHS[c]
        hw = width // 2
        base = STARTS[c]
        cols = pl.ds(base // 2, hw)
        for j, sign, q in ((0, 1, x_next), (1, -1, x_prev)):
            opp_in[c, j].wait_recv()
            lo = j * hw
            x_send[j, :, base + lo:base + lo + hw] = (
                block(c, q, lo, lo + hw) + opp_recv[j, :, cols].astype(F32)
            ).astype(BF16)
            lo = hw - lo
            x_send[j, :, base + lo:base + lo + hw] = block(c, q, lo, lo + hw).astype(BF16)
            full = pl.ds(base, width)
            q_in[c, j] = remote(x_send.at[j, :, full], x_recv.at[j, :, full], xdev(sign))

    def stage_z(c):
        width = WIDTHS[c]
        hw = width // 2
        base = STARTS[c]
        q_in[c, 0].wait_recv()
        q_in[c, 1].wait_recv()
        full = slice(base, base + width)
        summed = (
            block(c, x, 0, width)
            + x_recv[0, :, full].astype(F32) + x_recv[1, :, full].astype(F32)
        ).reshape(NZ, QTOK, width)
        part[c % SLOTS, :, x, :, 0:width] = summed
        cols = pl.ds(base // 2, hw)
        z_send[:, :, cols] = jnp.concatenate(
            [summed[:, :, :hw], summed[:, :, hw:]], axis=1
        ).astype(BF16)
        for k in range(1, NZ):
            z_part[c, k] = remote(
                z_send.at[rot(dp, k, NZ), :, cols], z_recv.at[k, :, cols], zdev(k)
            )
        q_out[:, full] = part[c % SLOTS, dp, x, :, 0:width]

    def stage_out(c):
        hw = WIDTHS[c] // 2
        acc = None
        for k in range(1, NZ):
            z_part[c, k].wait_recv()
            term = z_recv[k, :, pl.ds(STARTS[c] // 2, hw)].astype(F32)
            acc = term if acc is None else acc + term
        for j in range(2):
            cols = pl.ds(STARTS[c] + j * hw, hw)
            q_out[:, cols] = (q_out[:, cols] + acc[j * QTOK:(j + 1) * QTOK]) * D ** (-0.5)

    for t in range(NCHUNK):
        stage_matmul(t)
        if t == 0:
            for c in range(4, NCHUNK):
                refresh(c)
            outs = [
                pltpu.make_async_copy(w_buf, w_out, local_sem.at[4]),
                pltpu.make_async_copy(grad, s_out, local_sem.at[5]),
            ]
            for copy in outs:
                copy.start()
        if t >= 1:
            stage_relay(t - 1)
        if t >= 3:
            stage_z(t - 3)
        if t >= 5:
            stage_out(t - 5)
    stage_relay(NCHUNK - 1)
    for t in range(NCHUNK - 3, NCHUNK):
        stage_z(t)
    for t in range(NCHUNK - 5, NCHUNK):
        stage_out(t)

    for copy in outs:
        copy.wait()
    for copy in sent:
        copy.wait_send()
    assert count[0] <= N_SEM


def finish(*refs):
    src, dst, buf, sem = refs[:5], refs[5:10], refs[10:15], refs[15]
    views = []
    for i in range(2):
        for r in range(6):
            views.append((i, pl.ds(r * 48, 48)))
    views += [(i, slice(None)) for i in range(2, 5)]
    into = [
        pltpu.make_async_copy(src[i].at[rows], buf[i].at[rows], sem.at[0, n])
        for n, (i, rows) in enumerate(views)
    ]
    out = [
        pltpu.make_async_copy(buf[i].at[rows], dst[i].at[rows], sem.at[1, n])
        for n, (i, rows) in enumerate(views)
    ]
    for copy in into:
        copy.start()
    for first, second in zip(into, out):
        first.wait()
        second.start()
    for copy in out:
        copy.wait()


def body(weight, activations, cotangent, row_old, col_old, next_input):
    vm = pl.BlockSpec(memory_space=pltpu.VMEM)
    hbm = pl.BlockSpec(memory_space=pl.ANY)
    v = pltpu.VMEM

    def shape(*dims):
        return jax.ShapeDtypeStruct(dims, F32)

    new_weight, scaled_step, queries, row_factor, col_factor = pl.pallas_call(
        kernel,
        out_shape=(
            shape(FEAT, COLS), shape(FEAT, COLS), shape(QTOK, COLS), shape(FEAT),
            shape(1, COLS),
        ),
        in_specs=[hbm, hbm, hbm, hbm, vm, vm],
        out_specs=(hbm, hbm, vm, vm, vm),
        scratch_shapes=[
            v((FEAT, 128), F32),
            v((1, COLS), F32),
            v((TOKENS, COLS), BF16),
            v((FEAT, COLS), F32),
            v((FEAT, COLS), F32),
            v((TOK, BLOCK), BF16),
            v((NZ, TOK, FEAT), BF16),
            v((TOKENS, FEAT), BF16),
            v((FEAT, EARLY), BF16),
            v((FEAT, LATE), BF16),
            v((TOK, BLOCK), BF16),
            v((NZ, TOK, FEAT), BF16),
            v((NZ, HALF // 2, FEAT), BF16),
            v((2, NZ, HALF, FEAT), BF16),
            v((FEAT, 128), F32),
            v((8, FEAT), F32),
            v((4, 8, FEAT), F32),
            v((NZ, 8, 128), F32),
            v((NZ, 8, 128), F32),
            v((PLANE, 8, 128), F32),
            v((NZ, 8, 128), F32),
            v((8, 128), F32),
            v((FEAT, WIDTHS[0]), F32),
            v((FEAT, WIDTHS[0]), F32),
            v((8, FEAT), F32),
            v((8, FEAT), F32),
            v((FEAT, COLS), BF16),
            v((FEAT, COLS), BF16),
            v((SLOTS, NZ, NX, QTOK, WMAX), F32),
            v((2, TOK, COLS // 2), BF16),
            v((2, TOK, COLS // 2), BF16),
            v((2, TOK, COLS), BF16),
            v((2, TOK, COLS), BF16),
            v((NZ, 2 * QTOK, COLS // 2), BF16),
            v((NZ, 2 * QTOK, COLS // 2), BF16),
            pltpu.SemaphoreType.DMA((6,)),
            pltpu.SemaphoreType.DMA((N_SEM,)),
            pltpu.SemaphoreType.DMA((N_SEM,)),
        ],
        compiler_params=pltpu.CompilerParams(
            collective_id=0, has_side_effects=True, vmem_limit_bytes=60 * 1024 * 1024
        ),
        cost_estimate=pl.CostEstimate(
            flops=4 * TOKENS * FEAT * COLS, bytes_accessed=16_000_000, transcendentals=0
        ),
        name="update",
    )(
        cotangent, activations, next_input, weight,
        row_old.reshape(D // 128, 128), col_old.reshape(QW // 128, 128),
    )
    shapes = (
        shape(FEAT, COLS), shape(FEAT, COLS), shape(QTOK, COLS), shape(FEAT),
        shape(1, COLS),
    )
    new_weight, scaled_step, queries, row_factor, col_factor = pl.pallas_call(
        finish,
        in_specs=[hbm] * 5,
        out_specs=(hbm,) * 5,
        out_shape=shapes,
        scratch_shapes=[*(v(a.shape, F32) for a in shapes), pltpu.SemaphoreType.DMA((2, 15))],
        compiler_params=pltpu.CompilerParams(vmem_limit_bytes=60 * 1024 * 1024),
        cost_estimate=pl.CostEstimate(
            flops=0, bytes_accessed=16 * FEAT * COLS, transcendentals=0
        ),
        name="finish",
    )(new_weight, scaled_step, queries, row_factor, col_factor)
    return (
        new_weight, row_factor, col_factor.reshape(COLS), queries, scaled_step,
    )


def solution(mesh):
    placed = (
        P(("mrow", "dp"), "mcol"),
        P("dp", "mrow"),
        P("dp", "mcol"),
        P(),
        P(),
        P("dp", "mrow"),
    )
    return jax.shard_map(
        body,
        mesh=mesh,
        in_specs=placed,
        out_specs=(
            P(("mrow", "dp"), "mcol"),
            P(("mrow", "dp")),
            P("mcol"),
            P(("dp", "mrow"), "mcol"),
            P(("mrow", "dp"), "mcol"),
        ),
        check_vma=False,
    )
```
